128 devices in a mesh: facet: 16 (over y_hi, x, core), dp: 8 (over z, y_lo).
Axes of the slice: x: 4, y: 4 (y_hi: 2, y_lo: 2; y = y_hi * 2 + y_lo), z: 4, core: 2. Of those that a mesh axis runs over, the one named last changes fastest.
Arguments:
- sky_image: float32 [128, 1024, 256], P('dp', 'facet'), as said below
- wave_dual: float32 [128, 1024, 256], P('dp', 'facet'), may hold values from -3 to 3
- rank_dual: float32 [128, 1024, 256], P('dp', 'facet'), may hold values from -3 to 3
- data_dual: float32 [16, 16, 1024, 256], P('facet', 'dp'), may hold values from -3 to 3
- observed: bfloat16 [16, 16, 1024, 256], P('facet', 'dp'), may hold values from -6 to 6
- radius: float32 [16, 16, 256], P('facet', 'dp'), may hold values from 20 to 400
- degrid: bfloat16 [16, 16, 24, 1024, 128], P('facet', 'dp'), may hold values from -0.15625 to 0.15625
- tile_list: int32 [16, 16, 24], P(None, 'dp'), may hold values from 0 to 127, as said below
- counts: int32 [16, 16], P(None, 'dp'), may hold values from 6 to 24
- keep_count: int32 [16], P('facet'), may hold values from 2 to 64
Outputs:
- sky_next: float32 [128, 1024, 256], P('dp', 'facet')
- wave_next: float32 [128, 1024, 256], P('dp', 'facet')
- rank_next: float32 [128, 1024, 256], P('dp', 'facet')
- data_next: float32 [16, 16, 1024, 256], P('facet', 'dp')
The draws below stay inside these ranges and needn't reach their ends.
Inputs may be any that keep to these rules, and one draw needn't show every extreme that they name: `sky_image`: nonnegative. `tile_list`: A slot's value is f * 8 + t, tile t of source facet f in the block's band. Among the live slots of the 2 blocks of one device (facet g, band d) at most 3 name one source facet; in every band some source facet is named by exactly 3 live slots of every device of that band.
All inputs are finite; a program needn't handle non-finite values.
Results may differ from the reference program's by a relative error of at most 0.005.
Values may be sent and summed in bfloat16 or wider, within the bound.
A program may use at most 128 MiB of HBM per device.

```python
import math
import jax
import jax.numpy as jnp
from jax import lax

L = 256
TR = 8
TC = 16
HB = 16
WB = 64
NB = 2
KMAX = 24
VIS2 = 1024
FACETS = 16
BANDBLOCKS = 16
ROWS = 128
COLS = 1024
NT = 8
CAP = 3
N_DP = 8


def routing(key):
    key_count, key_spot, key_hot, key_perm, key_tile, key_fill = jax.random.split(jax.random.fold_in(key, 11), 6)
    counts = jax.random.randint(key_count, (FACETS, BANDBLOCKS), KMAX // 4, KMAX + 1)
    spot = jax.random.randint(key_spot, (), 0, FACETS * BANDBLOCKS)
    flat_index = jnp.arange(FACETS * BANDBLOCKS).reshape(FACETS, BANDBLOCKS)
    counts = jnp.where(flat_index == spot, KMAX, counts).astype(jnp.int32)
    band_count = BANDBLOCKS // NB
    hot_source = jax.random.randint(key_hot, (band_count,), 0, FACETS)
    slot_count = NB * KMAX
    is_live = (jnp.arange(KMAX)[None, None, :] < counts[:, :, None]).reshape(FACETS, band_count, slot_count)
    live_order = jnp.cumsum(is_live.astype(jnp.int32), axis=2) - 1
    others = (FACETS - 1) * CAP
    perm_keys = jax.random.split(key_perm, FACETS * band_count)
    perms = jax.vmap(lambda subkey: jax.random.permutation(subkey, others))(perm_keys).reshape(FACETS, band_count, others)
    later = jnp.clip(live_order - CAP, 0, others - 1)
    picked = jnp.take_along_axis(perms, later, axis=2)
    relative = picked // CAP
    hot_grid = hot_source[None, :, None]
    spread = relative + (relative >= hot_grid).astype(jnp.int32)
    source = jnp.where(live_order < CAP, hot_grid, spread)
    filler = jax.random.randint(key_fill, source.shape, 0, FACETS)
    source = jnp.where(is_live, source, filler)
    local_tile = jax.random.randint(key_tile, source.shape, 0, NT)
    tiles = (source * NT + local_tile).reshape(FACETS, BANDBLOCKS, KMAX).astype(jnp.int32)
    return (counts, tiles)


def draw_counts(key, part):
    return routing(key)[0]


def draw_tile_list(key, part):
    return routing(key)[1]


def draw_keep_count(key, part):
    key_base, key_low, key_high = jax.random.split(jax.random.fold_in(key, 5), 3)
    keep = jax.random.randint(key_base, (FACETS,), 2, L // 4 + 1)
    low_spot = jax.random.randint(key_low, (), 0, FACETS)
    high_spot = (low_spot + 1 + jax.random.randint(key_high, (), 0, FACETS - 1)) % FACETS
    index = jnp.arange(FACETS)
    keep = jnp.where(index == low_spot, 2, keep)
    keep = jnp.where(index == high_spot, L // 4, keep)
    return keep.astype(jnp.int32)


def draw_sky_image(key, part):
    key_pix, key_chan, key_grain = jax.random.split(jax.random.fold_in(key, 3), 3)
    row_pos = jnp.arange(ROWS, dtype=jnp.float32)
    rising = 1.0 + 2.0 * row_pos / max(ROWS - 1, 1)
    pixel_scale = jnp.exp(jax.random.uniform(key_pix, (ROWS, COLS), jnp.float32, 0.0, math.log(10.0)))
    grain = jax.random.uniform(key_grain, (ROWS, COLS, L), jnp.float32, 0.5, 1.5)
    channel_scale = jnp.exp(jax.random.uniform(key_chan, (L,), jnp.float32, 0.0, math.log(10.0)))
    return 0.05 * (pixel_scale * rising[:, None])[:, :, None] * channel_scale[None, None, :] * grain


def levels(stream_key, shape, cuts, low, high):
    def one(position, parts):
        draws = jax.random.uniform(jax.random.fold_in(jax.random.fold_in(stream_key, 6), position), (parts,), jnp.float32, low / len(cuts), high / len(cuts))
        return jnp.repeat(jnp.exp(draws), shape[position] // parts).reshape((-1,) + (1,) * (len(shape) - position - 1))

    loudness = one(*cuts[0])
    for cut in cuts[1:]:
        loudness = loudness * one(*cut)
    return loudness


def gaussian(own_key, shape, scale, reach, cuts=(), held_as=jnp.bfloat16):
    level = levels(own_key, shape, cuts, -0.22, 0.18) if cuts else 1.0
    drawn = jax.random.normal(own_key, shape, jnp.float32) * scale * level
    return jnp.minimum(jnp.maximum(drawn, -reach), reach).astype(held_as)


def setup_inputs(seed: int = 0) -> dict:
    key_list = jax.random.split(jax.random.key(seed), 11)
    sky_image = draw_sky_image(jax.random.fold_in(key_list[10], 71), 0)
    wave_dual = gaussian(key_list[1], (ROWS, COLS, L), 0.5, 3.0, ((0, 8), (1, 16)), jnp.float32)
    rank_dual = gaussian(key_list[2], (ROWS, COLS, L), 0.5, 3.0, ((0, 8), (1, 16)), jnp.float32)
    data_dual = gaussian(key_list[3], (FACETS, BANDBLOCKS, VIS2, L), 0.5, 3.0, ((0, 16), (1, 8)), jnp.float32)
    observed = gaussian(key_list[4], (FACETS, BANDBLOCKS, VIS2, L), 1.0, 6.0, ((0, 16), (1, 8)))
    radius = jnp.clip(jnp.exp(math.log(400.0) - 2.9957323 * jax.random.uniform(key_list[5], (FACETS, BANDBLOCKS, L), jnp.float32) ** levels(key_list[5], (FACETS, BANDBLOCKS, L), ((0, 16), (1, 8)), -0.2, 0.2)), 20.0, 400.0)
    degrid = gaussian(key_list[6], (FACETS, BANDBLOCKS, KMAX, VIS2, TR * TC), (TR * TC * KMAX // 2) ** -0.5, 0.15625, ((0, 16), (1, 8)))
    tile_list = draw_tile_list(jax.random.fold_in(key_list[10], 71), 0)
    counts = draw_counts(jax.random.fold_in(key_list[10], 71), 0)
    keep_count = draw_keep_count(jax.random.fold_in(key_list[10], 71), 0)
    return {"sky_image": sky_image, "wave_dual": wave_dual, "rank_dual": rank_dual, "data_dual": data_dual, "observed": observed, "radius": radius, "degrid": degrid, "tile_list": tile_list, "counts": counts, "keep_count": keep_count}


wavelet_taps = (-0.12940952255126037, -0.2241438680420134, 0.8365163037378079, -0.48296291314453416)
step_primal = 0.5
step_wave = 0.5
wave_bound = 1.0
step_rank = 0.5

def analysis(padded, height, columns):
    across = sum((wavelet_taps[offset] * padded[offset + 1:offset + 1 + height, :, :] for offset in range(4)))
    return sum((wavelet_taps[offset] * across[:, offset + 1:offset + 1 + columns, :] for offset in range(4)))

def synthesis(padded, height, columns):
    across = sum((wavelet_taps[offset] * padded[3 - offset:3 - offset + height, :, :] for offset in range(4)))
    return sum((wavelet_taps[offset] * across[:, 3 - offset:3 - offset + columns, :] for offset in range(4)))

def to_band_tiles(field):
    shaped = field.reshape(N_DP, HB // TR, TR, FACETS, WB // TC, TC, L)
    return shaped.transpose(0, 3, 1, 4, 2, 5, 6).reshape(N_DP, FACETS * NT, TR * TC, L)

def from_band_tiles(tiles):
    shaped = tiles.reshape(N_DP, FACETS, HB // TR, WB // TC, TR, TC, L)
    return shaped.transpose(0, 2, 4, 1, 3, 5, 6).reshape(ROWS, COLS, L)

def reference(sky_image, wave_dual, rank_dual, data_dual, observed, radius, degrid, tile_list, counts, keep_count):
    workers = FACETS * BANDBLOCKS
    is_live = jnp.arange(KMAX, dtype=jnp.int32)[None, None, :] < counts[:, :, None]
    flat_degrid = degrid.reshape(workers, KMAX, VIS2, TR * TC)
    dual_half = data_dual.astype(jnp.bfloat16).reshape(workers, VIS2, L)
    flat_tiles = tile_list.reshape(workers, KMAX).astype(jnp.int32)
    flat_live = is_live.reshape(workers, KMAX)
    band_of = jnp.arange(workers, dtype=jnp.int32) % BANDBLOCKS // NB

    def adjoint_step(back_band, inputs):
        weights, dual_rows, tiles, live_mask, band = inputs
        contrib = jnp.einsum('kvp,vl->kpl', weights.astype(jnp.float32), dual_rows.astype(jnp.float32)).astype(jnp.bfloat16)
        contrib = jnp.where(live_mask[:, None, None], contrib.astype(jnp.float32), jnp.float32(0.0))
        return (back_band.at[band, tiles].add(contrib), None)
    start_band = jnp.zeros((N_DP, FACETS * NT, TR * TC, L), jnp.float32)
    back_band, unused_out = lax.scan(adjoint_step, start_band, (flat_degrid, dual_half, flat_tiles, flat_live, band_of))
    back = from_band_tiles(back_band)
    wave_pad = jnp.pad(wave_dual, ((2, 2), (2, 2), (0, 0)))
    gradient = back + synthesis(wave_pad, ROWS, COLS) + rank_dual
    sky_next = jnp.maximum(sky_image - step_primal * gradient, 0.0)
    extrap = 2.0 * sky_next - sky_image
    bar_pad = jnp.pad(extrap, ((2, 2), (2, 2), (0, 0)))
    wave_next = jnp.clip(wave_dual + step_wave * analysis(bar_pad, ROWS, COLS), -wave_bound, wave_bound)
    mixed = rank_dual + step_rank * extrap
    facet_view = mixed.reshape(ROWS, FACETS, WB, L).transpose(1, 0, 2, 3).reshape(FACETS, ROWS * WB, L)

    def rank_facet(inputs):
        view, kept = inputs
        gram = jnp.dot(view.T.astype(jnp.float32), view.astype(jnp.float32), precision=lax.Precision.HIGHEST, preferred_element_type=jnp.float32)
        level = (jnp.trace(gram) + 1e-06) / kept.astype(jnp.float32)
        factor = jnp.linalg.cholesky(gram + level * jnp.eye(L, dtype=jnp.float32))
        solved = jax.scipy.linalg.cho_solve((factor, True), view.T)
        return level * solved.T
    rank_view = lax.map(rank_facet, (facet_view, keep_count))
    rank_next = rank_view.reshape(FACETS, ROWS, WB, L).transpose(1, 0, 2, 3).reshape(ROWS, COLS, L)
    bar_tiles = to_band_tiles(extrap.astype(jnp.bfloat16))

    def forward_one(inputs):
        weights, tiles, live_mask, band = inputs
        chosen = bar_tiles[band, tiles]
        chosen = jnp.where(live_mask[:, None, None], chosen, jnp.zeros_like(chosen))
        return jnp.einsum('kvp,kpl->vl', weights.astype(jnp.float32), chosen.astype(jnp.float32))
    model = lax.map(forward_one, (flat_degrid, flat_tiles, flat_live, band_of)).reshape(FACETS, BANDBLOCKS, VIS2, L)
    misfit = data_dual + model - observed.astype(jnp.float32)
    size_norm = jnp.sqrt(lax.optimization_barrier(jnp.sum(misfit * misfit, axis=2)) + 1e-06)
    data_next = misfit * jnp.maximum(0.0, 1.0 - radius / size_norm)[:, :, None, :]
    return (sky_next, wave_next, rank_next, data_next)
```

```python
import jax
import jax.numpy as jnp
from jax import lax
from jax.experimental import pallas as pl
from jax.experimental.pallas import tpu as pltpu
from jax.sharding import PartitionSpec as P

MESH = pl.DeviceIdType.MESH
F32 = jnp.float32
BF16 = jnp.bfloat16
HIGH = lax.Precision.HIGHEST

TAPS = (-0.12940952255126037, -0.2241438680420134, 0.8365163037378079, -0.48296291314453416)
FACETS = 16
DP = 8
CAP = 3
SLOTS = 48
TILES = 8
PIX = 128
CH = 256
VIS = 1024
H = 16
W = 64
EDGE = 8


def newton_scales(kappa, steps):
    start = 2.0 / (1.0 + kappa)
    rho = (kappa - 1.0) / (kappa + 1.0)
    scales = []
    for _ in range(steps):
        scales.append(2.0 / (2.0 - rho * rho))
        rho = rho * rho / (2.0 - rho * rho)
    return start, scales


START, SCALES = newton_scales(65.0, 8)


def facet_at(i, me):
    y, x, c = me // 8, (me // 2) % 4, me % 2
    y = (y + 1 - i // 8) % 2
    x = (x + 1 + (i // 2) % 4) % 4
    c = (c + 1 - i % 2) % 2
    return (y * 4 + x) * 2 + c


def kernel(
    tab, keep, tvec, radius, sky_h, wave_h, rank_h, dual_h, obs_h, deg_h,
    sky_o, wave_o, rank_o, data_o,
    deg, dual, obs, sky, rank, wpad, epad, half, send1, recv1, send2, recv2, bar,
    acr, acr2, cols, synth, mixed, pick, gram, gpart, gsend, gfull, amat, inv, wnext, snext, rnext, misfit,
    lsem, osem, s1, r1, s2, r2, hs, hr, gs, gr, as_, ar,
):
    me = lax.axis_index("facet")
    dp = lax.axis_index("dp")

    def local(n, src, dst):
        copy = pltpu.make_async_copy(src, dst, lsem.at[n])
        copy.start()
        return copy

    get_wave = local(0, wave_h, wpad.at[pl.ds(2, H)])
    get_dual = local(1, dual_h, dual)
    get_deg = [
        local(2 + q, deg_h.at[pl.ds(q * 12, 12)], deg.at[pl.ds(q * 12, 12)]) for q in range(4)
    ]
    get_sky = local(6, sky_h, sky)
    get_rank = local(7, rank_h, rank)
    get_obs = local(8, obs_h, obs)

    barrier = pltpu.get_barrier_semaphore()

    def greet_facet(i, carry):
        pl.semaphore_signal(barrier, inc=1, device_id={"facet": facet_at(i, me)}, device_id_type=MESH)
        return carry

    def greet_dp(i, carry):
        pl.semaphore_signal(barrier, inc=1, device_id={"dp": (dp + 1 + i) % DP}, device_id_type=MESH)
        return carry

    lax.fori_loop(0, FACETS - 1, greet_facet, 0)
    lax.fori_loop(0, DP - 1, greet_dp, 0)

    row = lax.broadcasted_iota(jnp.int32, (TILES * 16, SLOTS * 16), 0)
    lane = lax.broadcasted_iota(jnp.int32, (TILES * 16, SLOTS * 16), 1)
    hit = (tvec[...] == row // 16) & (row % 16 == lane % 16)
    pick[...] = jnp.where(hit, 1.0, 0.0).astype(BF16)

    @pl.when(dp == 0)
    def _():
        wpad[0:2] = jnp.zeros((2, W, CH), F32)
        epad[0:1] = jnp.zeros((1, W, CH), F32)

    @pl.when(dp == DP - 1)
    def _():
        wpad[18:19] = jnp.zeros((1, W, CH), F32)
        epad[17:19] = jnp.zeros((2, W, CH), F32)

    @pl.when(me == 0)
    def _():
        cols[4:6] = jnp.zeros((2, H, CH), F32)
        cols[10:11] = jnp.zeros((1, H, CH), F32)

    @pl.when(me == FACETS - 1)
    def _():
        cols[6:7] = jnp.zeros((1, H, CH), F32)
        cols[12:14] = jnp.zeros((2, H, CH), F32)

    pl.semaphore_wait(barrier, FACETS - 1 + DP - 1)

    def hop(n, src, dst, axis, to):
        return pltpu.make_async_remote_copy(
            src_ref=src, dst_ref=dst, send_sem=hs.at[n], recv_sem=hr.at[n],
            device_id={axis: to}, device_id_type=MESH,
        )

    down, up = (dp + 1) % DP, (dp + DP - 1) % DP
    right, left = (me + 1) % FACETS, (me + FACETS - 1) % FACETS
    hops = (
        (hop(0, wpad.at[pl.ds(16, 2)], wpad.at[pl.ds(0, 2)], "dp", down), dp < DP - 1, dp > 0),
        (hop(1, wpad.at[pl.ds(2, 1)], wpad.at[pl.ds(18, 1)], "dp", up), dp > 0, dp < DP - 1),
        (hop(2, cols.at[pl.ds(0, 2)], cols.at[pl.ds(4, 2)], "facet", right), me < FACETS - 1, me > 0),
        (hop(3, cols.at[pl.ds(2, 1)], cols.at[pl.ds(6, 1)], "facet", left), me > 0, me < FACETS - 1),
        (hop(4, epad.at[pl.ds(16, 1)], epad.at[pl.ds(0, 1)], "dp", down), dp < DP - 1, dp > 0),
        (hop(5, epad.at[pl.ds(1, 2)], epad.at[pl.ds(17, 2)], "dp", up), dp > 0, dp < DP - 1),
        (hop(6, cols.at[pl.ds(7, 1)], cols.at[pl.ds(10, 1)], "facet", right), me < FACETS - 1, me > 0),
        (hop(7, cols.at[pl.ds(8, 2)], cols.at[pl.ds(12, 2)], "facet", left), me > 0, me < FACETS - 1),
    )

    def hop_start(n):
        copy, sends, _ = hops[n]

        @pl.when(sends)
        def _():
            copy.start()

    def hop_arrive(n):
        copy, _, receives = hops[n]

        @pl.when(receives)
        def _():
            copy.wait_recv()

    def hop_left(n):
        copy, sends, _ = hops[n]

        @pl.when(sends)
        def _():
            copy.wait_send()

    get_wave.wait()
    hop_start(0)
    hop_start(1)
    get_dual.wait()
    half[...] = dual[...].astype(BF16)
    for copy in get_deg:
        copy.wait()

    def out_1(to):
        return pltpu.make_async_remote_copy(
            src_ref=send1.at[pl.ds(to * CAP, CAP)], dst_ref=recv1.at[pl.ds(me * CAP, CAP)],
            send_sem=s1.at[to], recv_sem=r1.at[me], device_id={"facet": to}, device_id_type=MESH,
        )

    def in_1(source):
        return pltpu.make_async_remote_copy(
            src_ref=send1.at[pl.ds(source * CAP, CAP)], dst_ref=recv1.at[pl.ds(source * CAP, CAP)],
            send_sem=s1.at[source], recv_sem=r1.at[source], device_id={"facet": source},
            device_id_type=MESH,
        )

    def adjoint(i, carry):
        to = facet_at(i, me)
        for j in range(CAP):
            e = to * CAP + j
            weights = deg[tab[0, e]]
            rows = half[tab[6, e]]
            part = lax.dot_general(
                weights, rows, (((0,), (0,)), ((), ())), preferred_element_type=F32
            )
            send1[e] = (part * tab[1, e].astype(F32)).astype(BF16)

        @pl.when(i < FACETS - 1)
        def _():
            out_1(to).start()

        return carry

    lax.fori_loop(0, FACETS, adjoint, 0)
    recv1[pl.ds(me * CAP, CAP)] = send1[pl.ds(me * CAP, CAP)]

    hop_arrive(0)
    hop_arrive(1)

    def synth_rows(i, carry):
        total = TAPS[0] * wpad[i + 3]
        for a in range(1, 4):
            total = total + TAPS[a] * wpad[i + 3 - a]
        acr[i, EDGE : EDGE + W] = total
        return carry

    lax.fori_loop(0, H, synth_rows, 0)
    for q in range(2):
        cols[q] = acr[:, EDGE + W - 2 + q, :]
    cols[2] = acr[:, EDGE, :]
    hop_start(2)
    hop_start(3)
    get_sky.wait()
    get_rank.wait()
    hop_arrive(2)
    hop_arrive(3)
    for q in range(2):
        acr[:, EDGE - 2 + q, :] = cols[4 + q]
    acr[:, EDGE + W, :] = cols[6]

    def synth_cols(i, carry):
        total = TAPS[0] * acr[i, EDGE + 1 : EDGE + 1 + W]
        for a in range(1, 4):
            total = total + TAPS[a] * acr[i, EDGE + 1 - a : EDGE + 1 - a + W]
        synth[i] = total
        return carry

    lax.fori_loop(0, H, synth_cols, 0)

    def arrive_1(i, carry):
        in_1(facet_at(i, me)).wait_recv()
        return carry

    lax.fori_loop(0, FACETS - 1, arrive_1, 0)

    def update(i, carry):
        at = pl.multiple_of(i * 16, 16)
        tiles = recv1[:, pl.ds(at, 16), :].reshape(SLOTS * 16, CH)
        back = jnp.dot(pick[...], tiles, preferred_element_type=F32)
        for r in range(2):
            y = r * 8 + i
            held = sky[y]
            gradient = back[r * W : (r + 1) * W] + synth[y] + rank[y]
            after = jnp.maximum(held - 0.5 * gradient, 0.0)
            extrap = 2.0 * after - held
            snext[y] = after
            epad[y + 1] = extrap
            mixed[pl.ds(pl.multiple_of(y * W, W), W)] = rank[y] + 0.5 * extrap
            bar[r * 4 : r * 4 + 4, pl.ds(at, 16), :] = extrap.astype(BF16).reshape(4, 16, CH)
        return carry

    lax.fori_loop(0, 8, update, 0)
    put_sky = pltpu.make_async_copy(snext, sky_o, osem.at[0])
    put_sky.start()
    hop_start(4)
    hop_start(5)

    def out_2(to):
        return pltpu.make_async_remote_copy(
            src_ref=send2.at[pl.ds(to * CAP, CAP)], dst_ref=recv2.at[pl.ds(me * CAP, CAP)],
            send_sem=s2.at[to], recv_sem=r2.at[me], device_id={"facet": to}, device_id_type=MESH,
        )

    def in_2(source):
        return pltpu.make_async_remote_copy(
            src_ref=send2.at[pl.ds(source * CAP, CAP)], dst_ref=recv2.at[pl.ds(source * CAP, CAP)],
            send_sem=s2.at[source], recv_sem=r2.at[source], device_id={"facet": source},
            device_id_type=MESH,
        )

    def deal(i, carry):
        to = facet_at(i, me)
        for j in range(CAP):
            send2[to * CAP + j] = bar[tab[2, to * CAP + j]]

        @pl.when(i < FACETS - 1)
        def _():
            out_2(to).start()

        return carry

    lax.fori_loop(0, FACETS, deal, 0)
    recv2[pl.ds(me * CAP, CAP)] = send2[pl.ds(me * CAP, CAP)]

    rows_d = CH // DP
    gram[...] = lax.dot_general(
        mixed[...], mixed[...], (((0,), (0,)), ((), ())), precision=HIGH, preferred_element_type=F32
    ).reshape(DP, rows_d, CH)

    def gram_out(to):
        return pltpu.make_async_remote_copy(
            src_ref=gram.at[to], dst_ref=gpart.at[dp], send_sem=gs.at[to], recv_sem=gr.at[dp],
            device_id={"dp": to}, device_id_type=MESH,
        )

    def gram_in(source):
        return pltpu.make_async_remote_copy(
            src_ref=gram.at[source], dst_ref=gpart.at[source], send_sem=gs.at[source],
            recv_sem=gr.at[source], device_id={"dp": source}, device_id_type=MESH,
        )

    def all_out(to):
        return pltpu.make_async_remote_copy(
            src_ref=gsend, dst_ref=gfull.at[dp], send_sem=as_.at[to], recv_sem=ar.at[dp],
            device_id={"dp": to}, device_id_type=MESH,
        )

    def all_in(source):
        return pltpu.make_async_remote_copy(
            src_ref=gsend, dst_ref=gfull.at[source], send_sem=as_.at[source],
            recv_sem=ar.at[source], device_id={"dp": source}, device_id_type=MESH,
        )

    def others(fn):
        def step(i, carry):
            fn((dp + 1 + i) % DP)
            return carry

        lax.fori_loop(0, DP - 1, step, 0)

    others(lambda d: gram_out(d).start())
    gpart[dp] = gram[dp]

    hop_arrive(4)
    hop_arrive(5)

    def analysis_rows(i, carry):
        total = TAPS[0] * epad[i]
        for a in range(1, 4):
            total = total + TAPS[a] * epad[i + a]
        acr2[i, EDGE : EDGE + W] = total
        return carry

    lax.fori_loop(0, H, analysis_rows, 0)
    cols[7] = acr2[:, EDGE + W - 1, :]
    for q in range(2):
        cols[8 + q] = acr2[:, EDGE + q, :]
    hop_start(6)
    hop_start(7)

    others(lambda d: gram_in(d).wait_recv())
    total = gpart[0]
    for d in range(1, DP):
        total = total + gpart[d]
    gsend[...] = total
    others(lambda d: all_out(d).start())
    gfull[dp] = total

    hop_arrive(6)
    hop_arrive(7)
    acr2[:, EDGE - 1, :] = cols[10]
    for q in range(2):
        acr2[:, EDGE + W + q, :] = cols[12 + q]

    def analysis_cols(i, carry):
        total = TAPS[0] * acr2[i, EDGE - 1 : EDGE - 1 + W]
        for a in range(1, 4):
            total = total + TAPS[a] * acr2[i, EDGE - 1 + a : EDGE - 1 + a + W]
        wnext[i] = jnp.clip(wpad[i + 2] + 0.5 * total, -1.0, 1.0)
        return carry

    lax.fori_loop(0, H, analysis_cols, 0)
    put_wave = pltpu.make_async_copy(wnext, wave_o, osem.at[1])
    put_wave.start()

    others(lambda d: all_in(d).wait_recv())
    full = gfull[...].reshape(CH, CH)
    diag = lax.broadcasted_iota(jnp.int32, (CH, CH), 0) == lax.broadcasted_iota(jnp.int32, (CH, CH), 1)
    eye = jnp.where(diag, 1.0, 0.0)
    trace = jnp.sum(jnp.sum(full * eye, axis=1, keepdims=True), axis=0, keepdims=True)
    level = (trace + 1e-06) / keep[0].astype(F32)
    matrix = eye + full / level
    amat[...] = matrix
    inv[...] = (SCALES[0] * START) * (2.0 * eye - START * matrix)
    for scale in SCALES[1:]:
        x = inv[...]
        residual = 2.0 * eye - jnp.dot(amat[...], x, precision=HIGH, preferred_element_type=F32)
        inv[...] = scale * jnp.dot(x, residual, precision=HIGH, preferred_element_type=F32)

    def apply_rank(i, carry):
        at = pl.ds(pl.multiple_of(i * 256, 256), 256)
        out = jnp.dot(mixed[at], inv[...], precision=HIGH, preferred_element_type=F32)
        rnext[pl.ds(i * 4, 4)] = out.reshape(4, W, CH)
        return carry

    lax.fori_loop(0, 4, apply_rank, 0)
    put_rank = pltpu.make_async_copy(rnext, rank_o, osem.at[2])
    put_rank.start()

    def arrive_2(i, carry):
        in_2(facet_at(i, me)).wait_recv()
        return carry

    lax.fori_loop(0, FACETS - 1, arrive_2, 0)
    get_obs.wait()

    def gather(s, carry):
        send2[s] = (recv2[tab[4, s]].astype(F32) * tab[5, s].astype(F32)).astype(BF16)
        return carry

    def left_2(i, carry):
        out_2(facet_at(i, me)).wait_send()
        return carry

    lax.fori_loop(0, FACETS - 1, left_2, 0)
    lax.fori_loop(0, SLOTS, gather, 0)
    half_slots = SLOTS // 2
    puts = []
    for b in range(2):
        def forward(i, total, b=b):
            at = pl.ds(pl.multiple_of(i * 256, 256), 256)
            weights = jnp.concatenate(
                [deg[b * half_slots + s, at, :] for s in range(half_slots)], axis=1
            )
            tiles = send2[b * half_slots : (b + 1) * half_slots].reshape(half_slots * PIX, CH)
            model = jnp.dot(weights, tiles, preferred_element_type=F32)
            miss = dual[b, at, :] + model - obs[b, at, :].astype(F32)
            misfit[b, at, :] = miss
            return total + jnp.sum(miss * miss, axis=0, keepdims=True)

        total = lax.fori_loop(0, 4, forward, jnp.zeros((1, CH), F32))
        size = jnp.sqrt(total + 1e-06)
        shrink = jnp.maximum(0.0, 1.0 - radius[pl.ds(b, 1), :] / size)

        def scale_rows(i, carry, b=b, shrink=shrink):
            at = pl.ds(pl.multiple_of(i * 128, 128), 128)
            misfit[b, at, :] = misfit[b, at, :] * shrink
            return carry

        lax.fori_loop(0, 8, scale_rows, 0)
        put = pltpu.make_async_copy(misfit.at[b], data_o.at[b], osem.at[3 + b])
        put.start()
        puts.append(put)

    def left_1(i, carry):
        out_1(facet_at(i, me)).wait_send()
        return carry

    lax.fori_loop(0, FACETS - 1, left_1, 0)
    others(lambda d: gram_out(d).wait_send())
    others(lambda d: all_out(d).wait_send())
    for n in range(8):
        hop_left(n)
    put_sky.wait()
    put_wave.wait()
    put_rank.wait()
    for put in puts:
        put.wait()


def routing(tile_list, counts, me):
    flat = tile_list.reshape(FACETS, SLOTS)
    live = (jnp.arange(24)[None, None, :] < counts[:, :, None]).reshape(FACETS, SLOTS)
    source = jnp.where(live, flat // TILES, -1)
    mine = lax.dynamic_slice_in_dim(source, me, 1, 0)
    match = jnp.concatenate([mine == jnp.arange(FACETS)[:, None], source == me], axis=0)
    slot = jnp.arange(SLOTS)
    before = jnp.sum(
        jnp.where(match[:, None, :] & (slot[None, None, :] < slot[None, :, None]), 1, 0), axis=2
    )
    chosen = match[:, None, :] & (before[:, None, :] == jnp.arange(CAP)[None, :, None])
    value = jnp.concatenate([jnp.broadcast_to(slot[None], (FACETS, SLOTS)), flat % TILES], axis=0)
    picked = jnp.sum(jnp.where(chosen, value[:, None, :], 0), axis=2)
    there = jnp.sum(jnp.where(chosen, 1, 0), axis=2)
    entry = jnp.sum(
        jnp.where(match[:FACETS], jnp.arange(FACETS)[:, None] * CAP + before[:FACETS], 0), axis=0
    )
    mine_live = jnp.sum(jnp.where(match[:FACETS], 1, 0), axis=0)
    slots = picked[:FACETS].reshape(SLOTS)
    tiles = picked[FACETS:].reshape(SLOTS)
    tiles_live = there[FACETS:].reshape(SLOTS)
    table = jnp.stack(
        [
            slots, there[:FACETS].reshape(SLOTS), tiles, tiles_live, entry, mine_live, slots // 24,
            jnp.zeros_like(slots),
        ]
    ).astype(jnp.int32)
    spread = jnp.repeat(jnp.where(tiles_live > 0, tiles, -1), 16)[None].astype(jnp.int32)
    return table, spread


def per_device(
    sky_image, wave_dual, rank_dual, data_dual, observed, radius, degrid, tile_list, counts, keep_count
):
    me = lax.axis_index("facet")
    table, spread = routing(tile_list, counts, me)
    hbm = pl.BlockSpec(memory_space=pl.ANY)
    vmem = pl.BlockSpec(memory_space=pltpu.VMEM)
    smem = pl.BlockSpec(memory_space=pltpu.SMEM)
    dma = pltpu.SemaphoreType.DMA
    image = jax.ShapeDtypeStruct((H, W, CH), F32)
    outs = pl.pallas_call(
        kernel,
        out_shape=(image, image, image, jax.ShapeDtypeStruct((2, VIS, CH), F32)),
        in_specs=[smem, smem, vmem, vmem] + [hbm] * 6,
        out_specs=[hbm] * 4,
        scratch_shapes=[
            pltpu.VMEM((SLOTS, VIS, PIX), BF16),
            pltpu.VMEM((2, VIS, CH), F32),
            pltpu.VMEM((2, VIS, CH), BF16),
            pltpu.VMEM((H, W, CH), F32),
            pltpu.VMEM((H, W, CH), F32),
            pltpu.VMEM((H + 3, W, CH), F32),
            pltpu.VMEM((H + 3, W, CH), F32),
            pltpu.VMEM((2, VIS, CH), BF16),
            pltpu.VMEM((SLOTS, PIX, CH), BF16),
            pltpu.VMEM((SLOTS, PIX, CH), BF16),
            pltpu.VMEM((SLOTS, PIX, CH), BF16),
            pltpu.VMEM((SLOTS, PIX, CH), BF16),
            pltpu.VMEM((TILES, PIX, CH), BF16),
            pltpu.VMEM((H, W + 2 * EDGE, CH), F32),
            pltpu.VMEM((H, W + 2 * EDGE, CH), F32),
            pltpu.VMEM((14, H, CH), F32),
            pltpu.VMEM((H, W, CH), F32),
            pltpu.VMEM((H * W, CH), F32),
            pltpu.VMEM((TILES * 16, SLOTS * 16), BF16),
            pltpu.VMEM((DP, CH // DP, CH), F32),
            pltpu.VMEM((DP, CH // DP, CH), F32),
            pltpu.VMEM((CH // DP, CH), F32),
            pltpu.VMEM((DP, CH // DP, CH), F32),
            pltpu.VMEM((CH, CH), F32),
            pltpu.VMEM((CH, CH), F32),
            pltpu.VMEM((H, W, CH), F32),
            pltpu.VMEM((H, W, CH), F32),
            pltpu.VMEM((H, W, CH), F32),
            pltpu.VMEM((2, VIS, CH), F32),
            dma((9,)),
            dma((5,)),
            dma((FACETS,)),
            dma((FACETS,)),
            dma((FACETS,)),
            dma((FACETS,)),
            dma((8,)),
            dma((8,)),
            dma((DP,)),
            dma((DP,)),
            dma((DP,)),
            dma((DP,)),
        ],
        compiler_params=pltpu.CompilerParams(
            collective_id=0, has_side_effects=True, vmem_limit_bytes=60 * 1024 * 1024
        ),
    )(
        table, keep_count, spread, radius[0], sky_image, wave_dual, rank_dual, data_dual[0],
        observed[0], degrid.reshape(SLOTS, VIS, PIX),
    )
    return outs[0], outs[1], outs[2], outs[3][None]


def solution(mesh):
    return jax.shard_map(
        per_device,
        mesh=mesh,
        in_specs=(
            P("dp", "facet", None),
            P("dp", "facet", None),
            P("dp", "facet", None),
            P("facet", "dp", None, None),
            P("facet", "dp", None, None),
            P("facet", "dp", None),
            P("facet", "dp", None, None, None),
            P(None, "dp", None),
            P(None, "dp"),
            P("facet"),
        ),
        out_specs=(
            P("dp", "facet", None),
            P("dp", "facet", None),
            P("dp", "facet", None),
            P("facet", "dp", None, None),
        ),
        check_vma=False,
    )
```

```python
import jax
import jax.numpy as jnp
from jax import lax
from jax.experimental import pallas as pl
from jax.experimental.pallas import tpu as pltpu
from jax.sharding import PartitionSpec as P

MESH = pl.DeviceIdType.MESH
F32 = jnp.float32
BF16 = jnp.bfloat16
HIGH = lax.Precision.HIGHEST

TAPS = (-0.12940952255126037, -0.2241438680420134, 0.8365163037378079, -0.48296291314453416)
FACETS = 16
DP = 8
CAP = 3
SLOTS = 48
TILES = 8
PIX = 128
CH = 256
VIS = 1024
H = 16
W = 64
HALF = 128
ROW = 8
EDGE = 8


def newton_scales(kappa, steps):
    start = 2.0 / (1.0 + kappa)
    rho = (kappa - 1.0) / (kappa + 1.0)
    scales = []
    for _ in range(steps):
        scales.append(2.0 / (2.0 - rho * rho))
        rho = rho * rho / (2.0 - rho * rho)
    return start, scales


START, SCALES = newton_scales(65.0, 8)


def column_at(i, me):
    x, c = (me // 2) % 4, me % 2
    return ((x + 1 + i // 2) % 4) * 2 + (c + 1 - i % 2) % 2


def match_table(source, value, target):
    lane = lax.broadcasted_iota(jnp.int32, (FACETS, SLOTS // 2), 1)
    seen = jnp.zeros((FACETS, 1), jnp.int32)
    values = [jnp.zeros((FACETS, 1), jnp.int32)] * CAP
    there = [jnp.zeros((FACETS, 1), jnp.int32)] * CAP
    for b in range(2):
        match = jnp.where(source[b] == target, 1, 0)
        before = jnp.broadcast_to(seen, match.shape)
        for s in range(SLOTS // 2 - 1):
            before = before + jnp.where(lane > s, match[:, s : s + 1], 0)
        seen = seen + jnp.sum(match, axis=1, keepdims=True)
        for j in range(CAP):
            chosen = jnp.where(before == j, match, 0)
            values[j] = values[j] + jnp.sum(chosen * value[b], axis=1, keepdims=True)
            there[j] = there[j] + jnp.sum(chosen, axis=1, keepdims=True)
    return values, there


def kernel(
    counts, keep, tiles_in, radius, sky_h, wave_h, rank_h, dual_h, obs_h, deg_h,
    sky_o, wave_o, rank_o, data_o,
    deg, dual, obs, sky, rank, wpad, epad, half, send1, recv1, ysend, yrecv, send2, recv2, bar, pbar_0, pbar_1,
    tcat, acc, acr, acr2, cols, synth, mixed, pick, tabv, tab, gram, gpart, gsend, gfull, amat, inv,
    lsem, s1, r1, s2, r2, ys, yr, hs, hr, gs, gr, as_, ar,
):
    me = lax.axis_index("facet")
    dp = lax.axis_index("dp")
    pbar = (pbar_0, pbar_1)
    mrow, mcol = me // ROW, me % ROW
    orow = 1 - mrow
    partner = orow * ROW + mcol

    def local(n, src, dst):
        copy = pltpu.make_async_copy(src, dst, lsem.at[n])
        copy.start()
        return copy

    get_wave = local(0, wave_h, wpad.at[pl.ds(2, H)])
    get_dual = local(1, dual_h, dual)
    get_deg = [
        local(2 + n, deg_h.at[pl.ds(n * 12, 12)], deg.at[pl.ds(n * 12, 12)]) for n in range(4)
    ]
    get_sky = local(6, sky_h, sky)
    get_rank = local(7, rank_h, rank)
    get_obs = local(8, obs_h, obs)

    barrier = pltpu.get_barrier_semaphore()

    def greet(axis, to):
        pl.semaphore_signal(barrier, inc=1, device_id={axis: to}, device_id_type=MESH)

    def greet_row(i, carry):
        greet("facet", mrow * ROW + column_at(i, me))
        return carry

    def greet_dp(i, carry):
        greet("dp", (dp + 1 + i) % DP)
        return carry

    down, up = (dp + 1) % DP, (dp + DP - 1) % DP
    right, left = (me + 1) % FACETS, (me + FACETS - 1) % FACETS
    lax.fori_loop(0, ROW - 1, greet_row, 0)
    lax.fori_loop(0, DP - 1, greet_dp, 0)
    greet("facet", partner)
    greet("facet", right)
    greet("facet", left)

    lane24 = lax.broadcasted_iota(jnp.int32, (1, SLOTS // 2), 1)
    rows16 = lax.broadcasted_iota(jnp.int32, (FACETS, 1), 0)
    mine, slot, workers, local_tile = [], [], [], []
    for b in range(2):
        line = tiles_in[pl.ds(me, 1), b, :]
        line = jnp.where(lane24 < counts[b, me], line // TILES, -1)
        mine.append(jnp.broadcast_to(line, (FACETS, SLOTS // 2)))
        slot.append(jnp.broadcast_to(lane24 + b * (SLOTS // 2), (FACETS, SLOTS // 2)))
        eight = tiles_in[pl.ds(pl.multiple_of(mrow * ROW, ROW), ROW), b, :]
        both = jnp.concatenate([eight, eight], axis=0)
        limit = jnp.zeros((FACETS, 1), jnp.int32)
        for n in range(ROW):
            limit = jnp.where(rows16 % ROW == n, counts[b, mrow * ROW + n], limit)
        workers.append(jnp.where(lane24 < limit, both // TILES, -1))
        local_tile.append(both % TILES)
    slots, slots_there = match_table(mine, slot, rows16)
    tiles, tiles_there = match_table(workers, local_tile, jnp.where(rows16 < ROW, partner, me))
    lanes = lax.broadcasted_iota(jnp.int32, (FACETS, 128), 1)
    table = jnp.zeros((FACETS, 128), jnp.int32)
    for n, column in enumerate(slots + slots_there + tiles + tiles_there):
        table = jnp.where(lanes == n, column, table)
    tabv[...] = table
    put_tab = pltpu.make_async_copy(tabv, tab, lsem.at[9])
    put_tab.start()

    wide = ROW * CAP * 16
    row = lax.broadcasted_iota(jnp.int32, (TILES * 16, wide), 0)
    lane = lax.broadcasted_iota(jnp.int32, (TILES * 16, wide), 1)
    lane8 = lax.broadcasted_iota(jnp.int32, (ROW, wide), 1)
    row8 = lax.broadcasted_iota(jnp.int32, (ROW, wide), 0)
    for kind in range(2):
        named = jnp.zeros((1, wide), jnp.int32)
        for j in range(CAP):
            code = jnp.where(tiles_there[j] > 0, tiles[j] + 1, 0)[kind * ROW : (kind + 1) * ROW]
            here = (lane8 // 48 == row8) & ((lane8 % 48) // 16 == j)
            named = named + jnp.sum(jnp.where(here, code, 0), axis=0, keepdims=True)
        hit = (named - 1 == row // 16) & (row % 16 == lane % 16)
        pick[kind] = jnp.where(hit, 1.0, 0.0).astype(BF16)

    @pl.when(dp == 0)
    def _():
        wpad[0:2] = jnp.zeros((2, W, CH), F32)
        epad[0:1] = jnp.zeros((1, W, CH), F32)

    @pl.when(dp == DP - 1)
    def _():
        wpad[18:19] = jnp.zeros((1, W, CH), F32)
        epad[17:19] = jnp.zeros((2, W, CH), F32)

    @pl.when(me == 0)
    def _():
        cols[4:6] = jnp.zeros((2, H, CH), F32)
        cols[10:11] = jnp.zeros((1, H, CH), F32)

    @pl.when(me == FACETS - 1)
    def _():
        cols[6:7] = jnp.zeros((1, H, CH), F32)
        cols[12:14] = jnp.zeros((2, H, CH), F32)

    pl.semaphore_wait(barrier, ROW - 1 + DP - 1 + 3)

    def hop(n, src, dst, axis, to):
        return pltpu.make_async_remote_copy(
            src_ref=src, dst_ref=dst, send_sem=hs.at[n], recv_sem=hr.at[n],
            device_id={axis: to}, device_id_type=MESH,
        )

    hops = (
        (hop(0, wpad.at[pl.ds(16, 2)], wpad.at[pl.ds(0, 2)], "dp", down), dp < DP - 1, dp > 0),
        (hop(1, wpad.at[pl.ds(2, 1)], wpad.at[pl.ds(18, 1)], "dp", up), dp > 0, dp < DP - 1),
        (hop(2, cols.at[pl.ds(0, 2)], cols.at[pl.ds(4, 2)], "facet", right), me < FACETS - 1, me > 0),
        (hop(3, cols.at[pl.ds(2, 1)], cols.at[pl.ds(6, 1)], "facet", left), me > 0, me < FACETS - 1),
        (hop(4, epad.at[pl.ds(16, 1)], epad.at[pl.ds(0, 1)], "dp", down), dp < DP - 1, dp > 0),
        (hop(5, epad.at[pl.ds(1, 2)], epad.at[pl.ds(17, 2)], "dp", up), dp > 0, dp < DP - 1),
        (hop(6, cols.at[pl.ds(7, 1)], cols.at[pl.ds(10, 1)], "facet", right), me < FACETS - 1, me > 0),
        (hop(7, cols.at[pl.ds(8, 2)], cols.at[pl.ds(12, 2)], "facet", left), me > 0, me < FACETS - 1),
    )

    def hop_start(n):
        copy, sends, _ = hops[n]

        @pl.when(sends)
        def _():
            copy.start()

    def hop_arrive(n):
        copy, _, receives = hops[n]

        @pl.when(receives)
        def _():
            copy.wait_recv()

    def hop_left(n):
        copy, sends, _ = hops[n]

        @pl.when(sends)
        def _():
            copy.wait_send()

    get_wave.wait()
    hop_start(0)
    hop_start(1)
    get_dual.wait()
    half[...] = dual[...].astype(BF16)
    put_tab.wait()
    for copy in get_deg:
        copy.wait()

    def row_copy(sends, src, dst, to, sent, came):
        return pltpu.make_async_remote_copy(
            src_ref=src, dst_ref=dst, send_sem=sends[0].at[sent], recv_sem=sends[1].at[came],
            device_id={"facet": mrow * ROW + to}, device_id_type=MESH,
        )

    def target_row(kind):
        return mrow if kind == 1 else orow

    def out_1(g, kind, to):
        return row_copy(
            (s1, r1), send1.at[g, pl.ds((target_row(kind) * ROW + to) * CAP, CAP)],
            recv1.at[g, pl.ds((kind * ROW + mcol) * CAP, CAP)], to,
            (g * 2 + kind) * ROW + to, (g * 2 + kind) * ROW + mcol,
        )

    def in_1(g, kind, source):
        region = recv1.at[g, pl.ds((kind * ROW + source) * CAP, CAP)]
        n = (g * 2 + kind) * ROW + source
        return row_copy((s1, r1), region, region, source, n, n)

    def out_2(g, kind, to):
        return row_copy(
            (s2, r2), send2.at[g, pl.ds((kind * ROW + to) * CAP, CAP)],
            recv2.at[g, pl.ds((target_row(kind) * ROW + mcol) * CAP, CAP)], to,
            (g * 2 + kind) * ROW + to, (g * 2 + kind) * ROW + mcol,
        )

    def in_2(g, kind, source):
        region = recv2.at[g, pl.ds((target_row(kind) * ROW + source) * CAP, CAP)]
        n = (g * 2 + kind) * ROW + source
        return row_copy((s2, r2), region, region, source, n, n)

    def across(g, n, src, dst):
        return pltpu.make_async_remote_copy(
            src_ref=src.at[g], dst_ref=dst, send_sem=ys.at[n * 2 + g], recv_sem=yr.at[n * 2 + g],
            device_id={"facet": partner}, device_id_type=MESH,
        )

    def each(fn):
        def step(i, carry):
            fn(column_at(i, me))
            return carry

        lax.fori_loop(0, ROW - 1, step, 0)

    for kind in range(2):
        def adjoint(i, carry, kind=kind):
            to = column_at(i, me)
            facet = target_row(kind) * ROW + to
            for j in range(CAP):
                at = tab[facet, j]
                part = lax.dot_general(
                    deg[at], half[jnp.where(at < SLOTS // 2, 0, 1)],
                    (((0,), (0,)), ((), ())), preferred_element_type=F32,
                )
                part = (part * tab[facet, CAP + j].astype(F32)).astype(BF16)
                send1[0, facet * CAP + j] = part[:, :HALF]
                send1[1, facet * CAP + j] = part[:, HALF:]

            @pl.when(i < ROW - 1)
            def _():
                out_1(0, kind, to).start()

            return carry

        lax.fori_loop(0, ROW, adjoint, 0)
    for kind in range(2):
        each(lambda to, kind=kind: out_1(1, kind, to).start())
    for g in range(2):
        for kind in range(2):
            recv1[g, pl.ds((kind * ROW + mcol) * CAP, CAP)] = send1[
                g, pl.ds((target_row(kind) * ROW + mcol) * CAP, CAP)
            ]

    hop_arrive(0)
    hop_arrive(1)

    def synth_rows(i, carry):
        total = TAPS[0] * wpad[i + 3]
        for a in range(1, 4):
            total = total + TAPS[a] * wpad[i + 3 - a]
        acr[i, EDGE : EDGE + W] = total
        return carry

    lax.fori_loop(0, H, synth_rows, 0)
    for q in range(2):
        cols[q] = acr[:, EDGE + W - 2 + q, :]
    cols[2] = acr[:, EDGE, :]
    hop_start(2)
    hop_start(3)
    get_sky.wait()
    get_rank.wait()
    hop_arrive(2)
    hop_arrive(3)
    for q in range(2):
        acr[:, EDGE - 2 + q, :] = cols[4 + q]
    acr[:, EDGE + W, :] = cols[6]

    def synth_cols(i, carry):
        total = TAPS[0] * acr[i, EDGE + 1 : EDGE + 1 + W]
        for a in range(1, 4):
            total = total + TAPS[a] * acr[i, EDGE + 1 - a : EDGE + 1 - a + W]
        synth[i] = total
        return carry

    lax.fori_loop(0, H, synth_cols, 0)

    entries = ROW * CAP

    def relay(g):
        each(lambda source: in_1(g, 0, source).wait_recv())

        def step(i, carry):
            at = pl.ds(pl.multiple_of(i * 16, 16), 16)
            part = recv1[g, 0:entries, at, :].reshape(entries * 16, HALF)
            total = jnp.dot(pick[0], part, preferred_element_type=F32)
            ysend[g, :, at, :] = total.astype(BF16).reshape(TILES, 16, HALF)
            return carry

        lax.fori_loop(0, 8, step, 0)
        across(g, 0, ysend, yrecv.at[g]).start()

    def update(g):
        each(lambda source: in_1(g, 1, source).wait_recv())
        across(g, 0, ysend, yrecv.at[g]).wait_recv()
        ch = slice(g * HALF, (g + 1) * HALF)

        def step(i, carry):
            at = pl.ds(pl.multiple_of(i * 16, 16), 16)
            part = recv1[g, entries : 2 * entries, at, :].reshape(entries * 16, HALF)
            back = jnp.dot(pick[1], part, preferred_element_type=F32)
            back = back + yrecv[g, :, at, :].reshape(TILES * 16, HALF).astype(F32)
            for r in range(2):
                y = r * 8 + i
                held = sky[y, :, ch]
                gradient = back[r * W : (r + 1) * W] + synth[y, :, ch] + rank[y, :, ch]
                after = jnp.maximum(held - 0.5 * gradient, 0.0)
                extrap = 2.0 * after - held
                sky_o[y, :, ch] = after
                epad[y + 1, :, ch] = extrap
                mixed[pl.ds(pl.multiple_of(y * W, W), W), ch] = rank[y, :, ch] + 0.5 * extrap
                bar[g, r * 4 : r * 4 + 4, at, :] = extrap.astype(BF16).reshape(4, 16, HALF)
            return carry

        lax.fori_loop(0, 8, step, 0)
        across(g, 1, bar, pbar[g]).start()

    def deal(g, kind):
        held = bar.at[g] if kind == 1 else pbar[g]
        if kind == 0:
            across(g, 1, bar, pbar[g]).wait_recv()

        def step(i, carry):
            to = column_at(i, me)
            for j in range(CAP):
                tile = held[tab[kind * ROW + to, 2 * CAP + j]]
                send2[g, (kind * ROW + to) * CAP + j] = tile

            @pl.when(i < ROW - 1)
            def _():
                out_2(g, kind, to).start()

            return carry

        lax.fori_loop(0, ROW, step, 0)
        recv2[g, pl.ds((target_row(kind) * ROW + mcol) * CAP, CAP)] = send2[
            g, pl.ds((kind * ROW + mcol) * CAP, CAP)
        ]

    relay(0)
    update(0)
    deal(0, 1)
    relay(1)
    deal(0, 0)
    update(1)
    deal(1, 1)
    hop_start(4)
    hop_start(5)

    rows_d = CH // DP
    gram[...] = lax.dot_general(
        mixed[...], mixed[...], (((0,), (0,)), ((), ())), precision=HIGH, preferred_element_type=F32
    ).reshape(DP, rows_d, CH)

    def gram_out(to):
        return pltpu.make_async_remote_copy(
            src_ref=gram.at[to], dst_ref=gpart.at[dp], send_sem=gs.at[to], recv_sem=gr.at[dp],
            device_id={"dp": to}, device_id_type=MESH,
        )

    def gram_in(source):
        return pltpu.make_async_remote_copy(
            src_ref=gram.at[source], dst_ref=gpart.at[source], send_sem=gs.at[source],
            recv_sem=gr.at[source], device_id={"dp": source}, device_id_type=MESH,
        )

    def all_out(to):
        return pltpu.make_async_remote_copy(
            src_ref=gsend, dst_ref=gfull.at[dp], send_sem=as_.at[to], recv_sem=ar.at[dp],
            device_id={"dp": to}, device_id_type=MESH,
        )

    def all_in(source):
        return pltpu.make_async_remote_copy(
            src_ref=gsend, dst_ref=gfull.at[source], send_sem=as_.at[source],
            recv_sem=ar.at[source], device_id={"dp": source}, device_id_type=MESH,
        )

    def others(fn):
        def step(i, carry):
            fn((dp + 1 + i) % DP)
            return carry

        lax.fori_loop(0, DP - 1, step, 0)

    others(lambda d: gram_out(d).start())
    gpart[dp] = gram[dp]

    deal(1, 0)

    hop_arrive(4)
    hop_arrive(5)

    def analysis_rows(i, carry):
        total = TAPS[0] * epad[i]
        for a in range(1, 4):
            total = total + TAPS[a] * epad[i + a]
        acr2[i, EDGE : EDGE + W] = total
        return carry

    lax.fori_loop(0, H, analysis_rows, 0)
    cols[7] = acr2[:, EDGE + W - 1, :]
    for q in range(2):
        cols[8 + q] = acr2[:, EDGE + q, :]
    hop_start(6)
    hop_start(7)

    others(lambda d: gram_in(d).wait_recv())
    total = gpart[0]
    for d in range(1, DP):
        total = total + gpart[d]
    gsend[...] = total
    others(lambda d: all_out(d).start())
    gfull[dp] = total

    hop_arrive(6)
    hop_arrive(7)
    acr2[:, EDGE - 1, :] = cols[10]
    for q in range(2):
        acr2[:, EDGE + W + q, :] = cols[12 + q]

    def analysis_cols(i, carry):
        total = TAPS[0] * acr2[i, EDGE - 1 : EDGE - 1 + W]
        for a in range(1, 4):
            total = total + TAPS[a] * acr2[i, EDGE - 1 + a : EDGE - 1 + a + W]
        wave_o[i] = jnp.clip(wpad[i + 2] + 0.5 * total, -1.0, 1.0)
        return carry

    lax.fori_loop(0, H, analysis_cols, 0)

    def forward(g, kind):
        each(lambda source: in_2(g, kind, source).wait_recv())
        first = target_row(kind) * ROW

        def spread(i, carry):
            for j in range(CAP):
                at = tab[first + i, j]
                live = tab[first + i, CAP + j]
                tile = recv2[g, (first + i) * CAP + j].astype(F32)
                for b in range(2):
                    mask = live * (jnp.where(at < SLOTS // 2, 1 - b, b))
                    tcat[i * CAP + j, :, b * HALF : (b + 1) * HALF] = (
                        tile * mask.astype(F32)
                    ).astype(BF16)
            return carry

        lax.fori_loop(0, ROW, spread, 0)

        def multiply(i, carry):
            at = pl.ds(pl.multiple_of(i * 256, 256), 256)
            weights = jnp.concatenate(
                [deg[tab[first + n // CAP, n % CAP], at, :] for n in range(entries)], axis=1
            )
            product = jnp.dot(
                weights, tcat[...].reshape(entries * PIX, CH), preferred_element_type=F32
            )
            if kind == 1:
                acc[g, at, :] = product
                return carry
            product = acc[g, at, :] + product
            ch = slice(g * HALF, (g + 1) * HALF)
            squares = []
            for b in range(2):
                miss = (
                    dual[b, at, ch]
                    + product[:, b * HALF : (b + 1) * HALF]
                    - obs[b, at, ch].astype(F32)
                )
                data_o[b, at, ch] = miss
                squares.append(carry[b] + jnp.sum(miss * miss, axis=0, keepdims=True))
            return tuple(squares)

        if kind == 1:
            lax.fori_loop(0, 4, multiply, 0)
            return
        zero = jnp.zeros((1, HALF), F32)
        totals = lax.fori_loop(0, 4, multiply, (zero, zero))
        ch = slice(g * HALF, (g + 1) * HALF)
        for b in range(2):
            size = jnp.sqrt(totals[b] + 1e-06)
            shrink = jnp.maximum(0.0, 1.0 - radius[pl.ds(b, 1), ch] / size)

            def scale_rows(i, carry, b=b, shrink=shrink):
                at = pl.ds(pl.multiple_of(i * 128, 128), 128)
                data_o[b, at, ch] = data_o[b, at, ch] * shrink
                return carry

            lax.fori_loop(0, 8, scale_rows, 0)

    get_obs.wait()
    forward(0, 1)
    forward(0, 0)

    others(lambda d: all_in(d).wait_recv())
    full = gfull[...].reshape(CH, CH)
    diag = lax.broadcasted_iota(jnp.int32, (CH, CH), 0) == lax.broadcasted_iota(jnp.int32, (CH, CH), 1)
    eye = jnp.where(diag, 1.0, 0.0)
    trace = jnp.sum(jnp.sum(full * eye, axis=1, keepdims=True), axis=0, keepdims=True)
    level = (trace + 1e-06) / keep[0].astype(F32)
    matrix = eye + full / level
    amat[...] = matrix
    inv[...] = (SCALES[0] * START) * (2.0 * eye - START * matrix)
    for scale in SCALES[1:]:
        x = inv[...]
        residual = 2.0 * eye - jnp.dot(amat[...], x, precision=HIGH, preferred_element_type=F32)
        inv[...] = scale * jnp.dot(x, residual, precision=HIGH, preferred_element_type=F32)

    def apply_rank(i, carry):
        at = pl.ds(pl.multiple_of(i * 256, 256), 256)
        out = jnp.dot(mixed[at], inv[...], precision=HIGH, preferred_element_type=F32)
        rank_o[pl.ds(i * 4, 4)] = out.reshape(4, W, CH)
        return carry

    lax.fori_loop(0, 4, apply_rank, 0)

    forward(1, 1)
    forward(1, 0)

    for g in range(2):
        for kind in range(2):
            each(lambda to, g=g, kind=kind: out_1(g, kind, to).wait_send())
            each(lambda to, g=g, kind=kind: out_2(g, kind, to).wait_send())
        across(g, 0, ysend, yrecv.at[g]).wait_send()
        across(g, 1, bar, pbar[g]).wait_send()
    others(lambda d: gram_out(d).wait_send())
    others(lambda d: all_out(d).wait_send())
    for n in range(8):
        hop_left(n)


def per_device(
    sky_image, wave_dual, rank_dual, data_dual, observed, radius, degrid, tile_list, counts, keep_count
):
    hbm = pl.BlockSpec(memory_space=pl.ANY)
    vmem = pl.BlockSpec(memory_space=pltpu.VMEM)
    smem = pl.BlockSpec(memory_space=pltpu.SMEM)
    dma = pltpu.SemaphoreType.DMA
    outs = pl.pallas_call(
        kernel,
        out_shape=(
            pltpu.VMEM((H, W, CH), F32), pltpu.VMEM((H, W, CH), F32), pltpu.VMEM((H, W, CH), F32),
            pltpu.VMEM((2, VIS, CH), F32),
        ),
        in_specs=[smem, smem, vmem, vmem] + [hbm] * 6,
        out_specs=[vmem] * 4,
        scratch_shapes=[
            pltpu.VMEM((SLOTS, VIS, PIX), BF16),
            pltpu.VMEM((2, VIS, CH), F32),
            pltpu.VMEM((2, VIS, CH), BF16),
            pltpu.VMEM((H, W, CH), F32),
            pltpu.VMEM((H, W, CH), F32),
            pltpu.VMEM((H + 3, W, CH), F32),
            pltpu.VMEM((H + 3, W, CH), F32),
            pltpu.VMEM((2, VIS, CH), BF16),
            pltpu.VMEM((2, SLOTS, PIX, HALF), BF16),
            pltpu.VMEM((2, SLOTS, PIX, HALF), BF16),
            pltpu.VMEM((2, TILES, PIX, HALF), BF16),
            pltpu.VMEM((2, TILES, PIX, HALF), BF16),
            pltpu.VMEM((2, SLOTS, PIX, HALF), BF16),
            pltpu.VMEM((2, SLOTS, PIX, HALF), BF16),
            pltpu.VMEM((2, TILES, PIX, HALF), BF16),
            pltpu.VMEM((TILES, PIX, HALF), BF16),
            pltpu.VMEM((TILES, PIX, HALF), BF16),
            pltpu.VMEM((ROW * CAP, PIX, CH), BF16),
            pltpu.VMEM((2, VIS, CH), F32),
            pltpu.VMEM((H, W + 2 * EDGE, CH), F32),
            pltpu.VMEM((H, W + 2 * EDGE, CH), F32),
            pltpu.VMEM((14, H, CH), F32),
            pltpu.VMEM((H, W, CH), F32),
            pltpu.VMEM((H * W, CH), F32),
            pltpu.VMEM((2, TILES * 16, ROW * CAP * 16), BF16),
            pltpu.VMEM((FACETS, 128), jnp.int32),
            pltpu.SMEM((FACETS, 128), jnp.int32),
            pltpu.VMEM((DP, CH // DP, CH), F32),
            pltpu.VMEM((DP, CH // DP, CH), F32),
            pltpu.VMEM((CH // DP, CH), F32),
            pltpu.VMEM((DP, CH // DP, CH), F32),
            pltpu.VMEM((CH, CH), F32),
            pltpu.VMEM((CH, CH), F32),
            dma((10,)),
            dma((4 * ROW,)),
            dma((4 * ROW,)),
            dma((4 * ROW,)),
            dma((4 * ROW,)),
            dma((4,)),
            dma((4,)),
            dma((8,)),
            dma((8,)),
            dma((DP,)),
            dma((DP,)),
            dma((DP,)),
            dma((DP,)),
        ],
        compiler_params=pltpu.CompilerParams(
            collective_id=0, has_side_effects=True, vmem_limit_bytes=52 * 1024 * 1024
        ),
    )(
        counts.T, keep_count, tile_list, radius[0], sky_image, wave_dual, rank_dual, data_dual[0],
        observed[0], degrid.reshape(SLOTS, VIS, PIX),
    )
    return outs[0], outs[1], outs[2], outs[3][None]


def solution(mesh):
    return jax.shard_map(
        per_device,
        mesh=mesh,
        in_specs=(
            P("dp", "facet", None),
            P("dp", "facet", None),
            P("dp", "facet", None),
            P("facet", "dp", None, None),
            P("facet", "dp", None, None),
            P("facet", "dp", None),
            P("facet", "dp", None, None, None),
            P(None, "dp", None),
            P(None, "dp"),
            P("facet"),
        ),
        out_specs=(
            P("dp", "facet", None),
            P("dp", "facet", None),
            P("dp", "facet", None),
            P("facet", "dp", None, None),
        ),
        check_vma=False,
    )
```

```python
import jax
import jax.numpy as jnp
from jax import lax
from jax.experimental import pallas as pl
from jax.experimental.pallas import tpu as pltpu
from jax.sharding import PartitionSpec as P

MESH = pl.DeviceIdType.MESH
F32 = jnp.float32
BF16 = jnp.bfloat16
HIGH = lax.Precision.HIGHEST

TAPS = (-0.12940952255126037, -0.2241438680420134, 0.8365163037378079, -0.48296291314453416)
FACETS = 16
DP = 8
CAP = 3
SLOTS = 48
TILES = 8
PIX = 128
CH = 256
VIS = 1024
H = 16
W = 64
HALF = 128
ROW = 8
EDGE = 8


def newton_scales(kappa, steps):
    start = 2.0 / (1.0 + kappa)
    rho = (kappa - 1.0) / (kappa + 1.0)
    scales = []
    for _ in range(steps):
        scales.append(2.0 / (2.0 - rho * rho))
        rho = rho * rho / (2.0 - rho * rho)
    return start, scales


START, SCALES = newton_scales(65.0, 8)


def halves(x):
    high = x.astype(BF16)
    return high, (x - high.astype(F32)).astype(BF16)


def dot3(a, b):
    (ah, al), (bh, bl) = halves(a), halves(b)
    return (
        jnp.dot(ah, bl, preferred_element_type=F32)
        + jnp.dot(al, bh, preferred_element_type=F32)
        + jnp.dot(ah, bh, preferred_element_type=F32)
    )


def column_at(i, me):
    x, c = (me // 2) % 4, me % 2
    return ((x + 1 + i // 2) % 4) * 2 + (c + 1 - i % 2) % 2


def match_table(source, value, target):
    lane = lax.broadcasted_iota(jnp.int32, (FACETS, SLOTS // 2), 1)
    seen = jnp.zeros((FACETS, 1), jnp.int32)
    values = [jnp.zeros((FACETS, 1), jnp.int32)] * CAP
    there = [jnp.zeros((FACETS, 1), jnp.int32)] * CAP
    for b in range(2):
        match = jnp.where(source[b] == target, 1, 0)
        before = jnp.broadcast_to(seen, match.shape)
        for s in range(SLOTS // 2 - 1):
            before = before + jnp.where(lane > s, match[:, s : s + 1], 0)
        seen = seen + jnp.sum(match, axis=1, keepdims=True)
        for j in range(CAP):
            chosen = jnp.where(before == j, match, 0)
            values[j] = values[j] + jnp.sum(chosen * value[b], axis=1, keepdims=True)
            there[j] = there[j] + jnp.sum(chosen, axis=1, keepdims=True)
    return values, there


def kernel(
    counts, keep, tiles_in, radius, sky_h, wave_h, rank_h, dual_h, obs_h, deg_h,
    sky_o, wave_o, rank_o, data_o,
    deg, dual, obs, sky, rank, wpad, epad, half, send1, recv1, ysend, yrecv, send2, recv2, bar, pbar_0, pbar_1,
    tcat, acc, acr, acr2, cols, synth, mixed, pick, tabv, tab, gram, gpart, gsend, gfull, amat, inv,
    lsem, s1, r1, s2, r2, ys, yr, hs, hr, gs, gr, as_, ar,
):
    me = lax.axis_index("facet")
    dp = lax.axis_index("dp")
    pbar = (pbar_0, pbar_1)
    mrow, mcol = me // ROW, me % ROW
    orow = 1 - mrow
    partner = orow * ROW + mcol

    def local(n, src, dst):
        copy = pltpu.make_async_copy(src, dst, lsem.at[n])
        copy.start()
        return copy

    get_wave = local(0, wave_h, wpad.at[pl.ds(2, H)])
    get_dual = local(1, dual_h, dual)
    get_deg = [
        local(2 + n, deg_h.at[pl.ds(n * 12, 12)], deg.at[pl.ds(n * 12, 12)]) for n in range(4)
    ]
    get_sky = local(6, sky_h, sky)
    get_rank = local(7, rank_h, rank)
    get_obs = local(8, obs_h, obs)

    barrier = pltpu.get_barrier_semaphore()

    def greet(axis, to):
        pl.semaphore_signal(barrier, inc=1, device_id={axis: to}, device_id_type=MESH)

    def greet_row(i, carry):
        greet("facet", mrow * ROW + column_at(i, me))
        return carry

    def greet_dp(i, carry):
        greet("dp", (dp + 1 + i) % DP)
        return carry

    down, up = (dp + 1) % DP, (dp + DP - 1) % DP
    right, left = (me + 1) % FACETS, (me + FACETS - 1) % FACETS
    lax.fori_loop(0, ROW - 1, greet_row, 0)
    lax.fori_loop(0, DP - 1, greet_dp, 0)
    greet("facet", partner)
    greet("facet", right)
    greet("facet", left)

    lane24 = lax.broadcasted_iota(jnp.int32, (1, SLOTS // 2), 1)
    rows16 = lax.broadcasted_iota(jnp.int32, (FACETS, 1), 0)
    mine, slot, workers, local_tile = [], [], [], []
    for b in range(2):
        line = tiles_in[pl.ds(me, 1), b, :]
        line = jnp.where(lane24 < counts[b, me], line // TILES, -1)
        mine.append(jnp.broadcast_to(line, (FACETS, SLOTS // 2)))
        slot.append(jnp.broadcast_to(lane24 + b * (SLOTS // 2), (FACETS, SLOTS // 2)))
        eight = tiles_in[pl.ds(pl.multiple_of(mrow * ROW, ROW), ROW), b, :]
        both = jnp.concatenate([eight, eight], axis=0)
        limit = jnp.zeros((FACETS, 1), jnp.int32)
        for n in range(ROW):
            limit = jnp.where(rows16 % ROW == n, counts[b, mrow * ROW + n], limit)
        workers.append(jnp.where(lane24 < limit, both // TILES, -1))
        local_tile.append(both % TILES)
    slots, slots_there = match_table(mine, slot, rows16)
    tiles, tiles_there = match_table(workers, local_tile, jnp.where(rows16 < ROW, partner, me))
    lanes = lax.broadcasted_iota(jnp.int32, (FACETS, 128), 1)
    table = jnp.zeros((FACETS, 128), jnp.int32)
    for n, column in enumerate(slots + slots_there + tiles + tiles_there):
        table = jnp.where(lanes == n, column, table)
    tabv[...] = table
    put_tab = pltpu.make_async_copy(tabv, tab, lsem.at[9])
    put_tab.start()

    wide = ROW * CAP * 16
    row = lax.broadcasted_iota(jnp.int32, (TILES * 16, wide), 0)
    lane = lax.broadcasted_iota(jnp.int32, (TILES * 16, wide), 1)
    lane8 = lax.broadcasted_iota(jnp.int32, (ROW, wide), 1)
    row8 = lax.broadcasted_iota(jnp.int32, (ROW, wide), 0)
    for kind in range(2):
        named = jnp.zeros((1, wide), jnp.int32)
        for j in range(CAP):
            code = jnp.where(tiles_there[j] > 0, tiles[j] + 1, 0)[kind * ROW : (kind + 1) * ROW]
            here = (lane8 // 48 == row8) & ((lane8 % 48) // 16 == j)
            named = named + jnp.sum(jnp.where(here, code, 0), axis=0, keepdims=True)
        hit = (named - 1 == row // 16) & (row % 16 == lane % 16)
        pick[kind] = jnp.where(hit, 1.0, 0.0).astype(BF16)

    @pl.when(dp == 0)
    def _():
        wpad[0:2] = jnp.zeros((2, W, CH), F32)
        epad[0:1] = jnp.zeros((1, W, CH), F32)

    @pl.when(dp == DP - 1)
    def _():
        wpad[18:19] = jnp.zeros((1, W, CH), F32)
        epad[17:19] = jnp.zeros((2, W, CH), F32)

    @pl.when(me == 0)
    def _():
        cols[4:6] = jnp.zeros((2, H, CH), F32)
        cols[10:11] = jnp.zeros((1, H, CH), F32)

    @pl.when(me == FACETS - 1)
    def _():
        cols[6:7] = jnp.zeros((1, H, CH), F32)
        cols[12:14] = jnp.zeros((2, H, CH), F32)

    pl.semaphore_wait(barrier, ROW - 1 + DP - 1 + 3)

    def hop(n, src, dst, axis, to):
        return pltpu.make_async_remote_copy(
            src_ref=src, dst_ref=dst, send_sem=hs.at[n], recv_sem=hr.at[n],
            device_id={axis: to}, device_id_type=MESH,
        )

    hops = (
        (hop(0, wpad.at[pl.ds(16, 2)], wpad.at[pl.ds(0, 2)], "dp", down), dp < DP - 1, dp > 0),
        (hop(1, wpad.at[pl.ds(2, 1)], wpad.at[pl.ds(18, 1)], "dp", up), dp > 0, dp < DP - 1),
        (hop(2, cols.at[pl.ds(0, 2)], cols.at[pl.ds(4, 2)], "facet", right), me < FACETS - 1, me > 0),
        (hop(3, cols.at[pl.ds(2, 1)], cols.at[pl.ds(6, 1)], "facet", left), me > 0, me < FACETS - 1),
        (hop(4, epad.at[pl.ds(16, 1)], epad.at[pl.ds(0, 1)], "dp", down), dp < DP - 1, dp > 0),
        (hop(5, epad.at[pl.ds(1, 2)], epad.at[pl.ds(17, 2)], "dp", up), dp > 0, dp < DP - 1),
        (hop(6, cols.at[pl.ds(7, 1)], cols.at[pl.ds(10, 1)], "facet", right), me < FACETS - 1, me > 0),
        (hop(7, cols.at[pl.ds(8, 2)], cols.at[pl.ds(12, 2)], "facet", left), me > 0, me < FACETS - 1),
    )

    def hop_start(n):
        copy, sends, _ = hops[n]

        @pl.when(sends)
        def _():
            copy.start()

    def hop_arrive(n):
        copy, _, receives = hops[n]

        @pl.when(receives)
        def _():
            copy.wait_recv()

    def hop_left(n):
        copy, sends, _ = hops[n]

        @pl.when(sends)
        def _():
            copy.wait_send()

    get_wave.wait()
    hop_start(0)
    hop_start(1)
    get_dual.wait()
    half[...] = dual[...].astype(BF16)
    put_tab.wait()
    for copy in get_deg:
        copy.wait()

    def row_copy(sends, src, dst, to, sent, came):
        return pltpu.make_async_remote_copy(
            src_ref=src, dst_ref=dst, send_sem=sends[0].at[sent], recv_sem=sends[1].at[came],
            device_id={"facet": mrow * ROW + to}, device_id_type=MESH,
        )

    def target_row(kind):
        return mrow if kind == 1 else orow

    def out_1(g, kind, to):
        return row_copy(
            (s1, r1), send1.at[g, pl.ds((target_row(kind) * ROW + to) * CAP, CAP)],
            recv1.at[g, pl.ds((kind * ROW + mcol) * CAP, CAP)], to,
            (g * 2 + kind) * ROW + to, (g * 2 + kind) * ROW + mcol,
        )

    def in_1(g, kind, source):
        region = recv1.at[g, pl.ds((kind * ROW + source) * CAP, CAP)]
        n = (g * 2 + kind) * ROW + source
        return row_copy((s1, r1), region, region, source, n, n)

    def out_2(g, kind, to):
        return row_copy(
            (s2, r2), send2.at[g, pl.ds((kind * ROW + to) * CAP, CAP)],
            recv2.at[g, pl.ds((target_row(kind) * ROW + mcol) * CAP, CAP)], to,
            (g * 2 + kind) * ROW + to, (g * 2 + kind) * ROW + mcol,
        )

    def in_2(g, kind, source):
        region = recv2.at[g, pl.ds((target_row(kind) * ROW + source) * CAP, CAP)]
        n = (g * 2 + kind) * ROW + source
        return row_copy((s2, r2), region, region, source, n, n)

    def across(g, n, src, dst):
        return pltpu.make_async_remote_copy(
            src_ref=src.at[g], dst_ref=dst, send_sem=ys.at[n * 2 + g], recv_sem=yr.at[n * 2 + g],
            device_id={"facet": partner}, device_id_type=MESH,
        )

    def each(fn):
        def step(i, carry):
            fn(column_at(i, me))
            return carry

        lax.fori_loop(0, ROW - 1, step, 0)

    for kind in range(2):
        def adjoint(i, carry, kind=kind):
            to = column_at(i, me)
            facet = target_row(kind) * ROW + to
            for j in range(CAP):
                at = tab[facet, j]
                part = lax.dot_general(
                    deg[at], half[jnp.where(at < SLOTS // 2, 0, 1)],
                    (((0,), (0,)), ((), ())), preferred_element_type=F32,
                )
                part = (part * tab[facet, CAP + j].astype(F32)).astype(BF16)
                send1[0, facet * CAP + j] = part[:, :HALF]
                send1[1, facet * CAP + j] = part[:, HALF:]

            @pl.when(i < ROW - 1)
            def _():
                out_1(0, kind, to).start()

            return carry

        lax.fori_loop(0, ROW, adjoint, 0)
    for g in range(2):
        for kind in range(2):
            recv1[g, pl.ds((kind * ROW + mcol) * CAP, CAP)] = send1[
                g, pl.ds((target_row(kind) * ROW + mcol) * CAP, CAP)
            ]

    hop_arrive(0)
    hop_arrive(1)

    def synth_rows(i, carry):
        total = TAPS[0] * wpad[i + 3]
        for a in range(1, 4):
            total = total + TAPS[a] * wpad[i + 3 - a]
        acr[i, EDGE : EDGE + W] = total
        return carry

    lax.fori_loop(0, H, synth_rows, 0)
    for q in range(2):
        cols[q] = acr[:, EDGE + W - 2 + q, :]
    cols[2] = acr[:, EDGE, :]
    hop_start(2)
    hop_start(3)
    get_sky.wait()
    get_rank.wait()
    hop_arrive(2)
    hop_arrive(3)
    for q in range(2):
        acr[:, EDGE - 2 + q, :] = cols[4 + q]
    acr[:, EDGE + W, :] = cols[6]

    def synth_cols(i, carry):
        total = TAPS[0] * acr[i, EDGE + 1 : EDGE + 1 + W]
        for a in range(1, 4):
            total = total + TAPS[a] * acr[i, EDGE + 1 - a : EDGE + 1 - a + W]
        synth[i] = total
        return carry

    lax.fori_loop(0, H, synth_cols, 0)

    def follow(kind, to):
        out_1(0, kind, to).wait_send()
        out_1(1, kind, to).start()

    for kind in range(2):
        each(lambda to, kind=kind: follow(kind, to))

    entries = ROW * CAP

    def relay(g):
        each(lambda source: in_1(g, 0, source).wait_recv())

        def step(i, carry):
            at = pl.ds(pl.multiple_of(i * 16, 16), 16)
            part = recv1[g, 0:entries, at, :].reshape(entries * 16, HALF)
            total = jnp.dot(pick[0], part, preferred_element_type=F32)
            ysend[g, :, at, :] = total.astype(BF16).reshape(TILES, 16, HALF)
            return carry

        lax.fori_loop(0, 8, step, 0)
        across(g, 0, ysend, yrecv.at[g]).start()

    def update(g):
        each(lambda source: in_1(g, 1, source).wait_recv())
        across(g, 0, ysend, yrecv.at[g]).wait_recv()
        ch = slice(g * HALF, (g + 1) * HALF)

        def step(i, carry):
            at = pl.ds(pl.multiple_of(i * 16, 16), 16)
            part = recv1[g, entries : 2 * entries, at, :].reshape(entries * 16, HALF)
            back = jnp.dot(pick[1], part, preferred_element_type=F32)
            back = back + yrecv[g, :, at, :].reshape(TILES * 16, HALF).astype(F32)
            for r in range(2):
                y = r * 8 + i
                held = sky[y, :, ch]
                gradient = back[r * W : (r + 1) * W] + synth[y, :, ch] + rank[y, :, ch]
                after = jnp.maximum(held - 0.5 * gradient, 0.0)
                extrap = 2.0 * after - held
                sky_o[y, :, ch] = after
                epad[y + 1, :, ch] = extrap
                mixed[pl.ds(pl.multiple_of(y * W, W), W), ch] = rank[y, :, ch] + 0.5 * extrap
                bar[g, r * 4 : r * 4 + 4, at, :] = extrap.astype(BF16).reshape(4, 16, HALF)
            return carry

        lax.fori_loop(0, 8, step, 0)
        across(g, 1, bar, pbar[g]).start()

    def deal(g, kind):
        held = bar.at[g] if kind == 1 else pbar[g]
        if kind == 0:
            across(g, 1, bar, pbar[g]).wait_recv()

        def step(i, carry):
            to = column_at(i, me)
            for j in range(CAP):
                tile = held[tab[kind * ROW + to, 2 * CAP + j]]
                send2[g, (kind * ROW + to) * CAP + j] = tile

            @pl.when(i < ROW - 1)
            def _():
                out_2(g, kind, to).start()

            return carry

        lax.fori_loop(0, ROW, step, 0)
        recv2[g, pl.ds((target_row(kind) * ROW + mcol) * CAP, CAP)] = send2[
            g, pl.ds((kind * ROW + mcol) * CAP, CAP)
        ]

    def forward(g, kind):
        each(lambda source: in_2(g, kind, source).wait_recv())
        first = target_row(kind) * ROW

        def spread(i, carry):
            for j in range(CAP):
                at = tab[first + i, j]
                live = tab[first + i, CAP + j]
                tile = recv2[g, (first + i) * CAP + j].astype(F32)
                for b in range(2):
                    mask = live * (jnp.where(at < SLOTS // 2, 1 - b, b))
                    tcat[i * CAP + j, :, b * HALF : (b + 1) * HALF] = (
                        tile * mask.astype(F32)
                    ).astype(BF16)
            return carry

        lax.fori_loop(0, ROW, spread, 0)

        def multiply(i, carry):
            at = pl.ds(pl.multiple_of(i * 512, 512), 512)
            weights = jnp.concatenate(
                [deg[tab[first + n // CAP, n % CAP], at, :] for n in range(entries)], axis=1
            )
            product = jnp.dot(
                weights, tcat[...].reshape(entries * PIX, CH), preferred_element_type=F32
            )
            if kind == 1:
                acc[g, at, :] = product
                return carry
            product = acc[g, at, :] + product
            ch = slice(g * HALF, (g + 1) * HALF)
            squares = []
            for b in range(2):
                miss = (
                    dual[b, at, ch]
                    + product[:, b * HALF : (b + 1) * HALF]
                    - obs[b, at, ch].astype(F32)
                )
                data_o[b, at, ch] = miss
                squares.append(carry[b] + jnp.sum(miss * miss, axis=0, keepdims=True))
            return tuple(squares)

        if kind == 1:
            lax.fori_loop(0, 2, multiply, 0)
            return
        zero = jnp.zeros((1, HALF), F32)
        totals = lax.fori_loop(0, 2, multiply, (zero, zero))
        ch = slice(g * HALF, (g + 1) * HALF)
        for b in range(2):
            size = jnp.sqrt(totals[b] + 1e-06)
            shrink = jnp.maximum(0.0, 1.0 - radius[pl.ds(b, 1), ch] / size)

            def scale_rows(i, carry, b=b, shrink=shrink):
                at = pl.ds(pl.multiple_of(i * 128, 128), 128)
                data_o[b, at, ch] = data_o[b, at, ch] * shrink
                return carry

            lax.fori_loop(0, 8, scale_rows, 0)

    get_obs.wait()
    relay(0)
    update(0)
    deal(0, 1)
    relay(1)
    deal(0, 0)
    update(1)
    deal(1, 1)
    hop_start(4)
    hop_start(5)

    rows_d = CH // DP
    high, low = halves(mixed[...])
    first = lax.dot_general(high, high, (((0,), (0,)), ((), ())), preferred_element_type=F32)
    second = lax.dot_general(high, low, (((0,), (0,)), ((), ())), preferred_element_type=F32)
    gram[...] = (first + (second + second.T)).reshape(DP, rows_d, CH)

    def gram_out(to):
        return pltpu.make_async_remote_copy(
            src_ref=gram.at[to], dst_ref=gpart.at[dp], send_sem=gs.at[to], recv_sem=gr.at[dp],
            device_id={"dp": to}, device_id_type=MESH,
        )

    def gram_in(source):
        return pltpu.make_async_remote_copy(
            src_ref=gram.at[source], dst_ref=gpart.at[source], send_sem=gs.at[source],
            recv_sem=gr.at[source], device_id={"dp": source}, device_id_type=MESH,
        )

    def all_out(to):
        return pltpu.make_async_remote_copy(
            src_ref=gsend, dst_ref=gfull.at[dp], send_sem=as_.at[to], recv_sem=ar.at[dp],
            device_id={"dp": to}, device_id_type=MESH,
        )

    def all_in(source):
        return pltpu.make_async_remote_copy(
            src_ref=gsend, dst_ref=gfull.at[source], send_sem=as_.at[source],
            recv_sem=ar.at[source], device_id={"dp": source}, device_id_type=MESH,
        )

    def others(fn):
        def step(i, carry):
            fn((dp + 1 + i) % DP)
            return carry

        lax.fori_loop(0, DP - 1, step, 0)

    others(lambda d: gram_out(d).start())
    gpart[dp] = gram[dp]

    forward(0, 1)
    deal(1, 0)
    forward(0, 0)

    hop_arrive(4)
    hop_arrive(5)

    def analysis_rows(i, carry):
        total = TAPS[0] * epad[i]
        for a in range(1, 4):
            total = total + TAPS[a] * epad[i + a]
        acr2[i, EDGE : EDGE + W] = total
        return carry

    lax.fori_loop(0, H, analysis_rows, 0)
    cols[7] = acr2[:, EDGE + W - 1, :]
    for q in range(2):
        cols[8 + q] = acr2[:, EDGE + q, :]
    hop_start(6)
    hop_start(7)

    others(lambda d: gram_in(d).wait_recv())
    total = gpart[0]
    for d in range(1, DP):
        total = total + gpart[d]
    gsend[...] = total
    others(lambda d: all_out(d).start())
    gfull[dp] = total

    hop_arrive(6)
    hop_arrive(7)
    acr2[:, EDGE - 1, :] = cols[10]
    for q in range(2):
        acr2[:, EDGE + W + q, :] = cols[12 + q]

    def analysis_cols(i, carry):
        total = TAPS[0] * acr2[i, EDGE - 1 : EDGE - 1 + W]
        for a in range(1, 4):
            total = total + TAPS[a] * acr2[i, EDGE - 1 + a : EDGE - 1 + a + W]
        wave_o[i] = jnp.clip(wpad[i + 2] + 0.5 * total, -1.0, 1.0)
        return carry

    lax.fori_loop(0, H, analysis_cols, 0)

    others(lambda d: all_in(d).wait_recv())
    full = gfull[...].reshape(CH, CH)
    diag = lax.broadcasted_iota(jnp.int32, (CH, CH), 0) == lax.broadcasted_iota(jnp.int32, (CH, CH), 1)
    eye = jnp.where(diag, 1.0, 0.0)
    trace = jnp.sum(jnp.sum(full * eye, axis=1, keepdims=True), axis=0, keepdims=True)
    level = (trace + 1e-06) / keep[0].astype(F32)
    matrix = eye + full / level
    amat[...] = matrix
    inv[...] = (SCALES[0] * START) * (2.0 * eye - START * matrix)
    coarse = matrix.astype(BF16)
    x = inv[...]
    for scale in SCALES[1:5]:
        residual = 2.0 * eye - jnp.dot(coarse, x.astype(BF16), preferred_element_type=F32)
        x = scale * jnp.dot(x.astype(BF16), residual.astype(BF16), preferred_element_type=F32)
    inv[...] = x
    for _ in range(3):
        x = inv[...]
        residual = eye - dot3(amat[...], x)
        inv[...] = x + dot3(x, residual)

    def apply_rank(i, carry):
        at = pl.ds(pl.multiple_of(i * 256, 256), 256)
        out = dot3(mixed[at], inv[...])
        rank_o[pl.ds(i * 4, 4)] = out.reshape(4, W, CH)
        return carry

    lax.fori_loop(0, 4, apply_rank, 0)

    forward(1, 1)
    forward(1, 0)

    for g in range(2):
        for kind in range(2):
            if g == 1:
                each(lambda to, kind=kind: out_1(1, kind, to).wait_send())
            each(lambda to, g=g, kind=kind: out_2(g, kind, to).wait_send())
        across(g, 0, ysend, yrecv.at[g]).wait_send()
        across(g, 1, bar, pbar[g]).wait_send()
    others(lambda d: gram_out(d).wait_send())
    others(lambda d: all_out(d).wait_send())
    for n in range(8):
        hop_left(n)


def per_device(
    sky_image, wave_dual, rank_dual, data_dual, observed, radius, degrid, tile_list, counts, keep_count
):
    hbm = pl.BlockSpec(memory_space=pl.ANY)
    vmem = pl.BlockSpec(memory_space=pltpu.VMEM)
    smem = pl.BlockSpec(memory_space=pltpu.SMEM)
    dma = pltpu.SemaphoreType.DMA
    outs = pl.pallas_call(
        kernel,
        out_shape=(
            pltpu.VMEM((H, W, CH), F32), pltpu.VMEM((H, W, CH), F32), pltpu.VMEM((H, W, CH), F32),
            pltpu.VMEM((2, VIS, CH), F32),
        ),
        in_specs=[smem, smem, vmem, vmem] + [hbm] * 6,
        out_specs=[vmem] * 4,
        scratch_shapes=[
            pltpu.VMEM((SLOTS, VIS, PIX), BF16),
            pltpu.VMEM((2, VIS, CH), F32),
            pltpu.VMEM((2, VIS, CH), BF16),
            pltpu.VMEM((H, W, CH), F32),
            pltpu.VMEM((H, W, CH), F32),
            pltpu.VMEM((H + 3, W, CH), F32),
            pltpu.VMEM((H + 3, W, CH), F32),
            pltpu.VMEM((2, VIS, CH), BF16),
            pltpu.VMEM((2, SLOTS, PIX, HALF), BF16),
            pltpu.VMEM((2, SLOTS, PIX, HALF), BF16),
            pltpu.VMEM((2, TILES, PIX, HALF), BF16),
            pltpu.VMEM((2, TILES, PIX, HALF), BF16),
            pltpu.VMEM((2, SLOTS, PIX, HALF), BF16),
            pltpu.VMEM((2, SLOTS, PIX, HALF), BF16),
            pltpu.VMEM((2, TILES, PIX, HALF), BF16),
            pltpu.VMEM((TILES, PIX, HALF), BF16),
            pltpu.VMEM((TILES, PIX, HALF), BF16),
            pltpu.VMEM((ROW * CAP, PIX, CH), BF16),
            pltpu.VMEM((2, VIS, CH), F32),
            pltpu.VMEM((H, W + 2 * EDGE, CH), F32),
            pltpu.VMEM((H, W + 2 * EDGE, CH), F32),
            pltpu.VMEM((14, H, CH), F32),
            pltpu.VMEM((H, W, CH), F32),
            pltpu.VMEM((H * W, CH), F32),
            pltpu.VMEM((2, TILES * 16, ROW * CAP * 16), BF16),
            pltpu.VMEM((FACETS, 128), jnp.int32),
            pltpu.SMEM((FACETS, 128), jnp.int32),
            pltpu.VMEM((DP, CH // DP, CH), F32),
            pltpu.VMEM((DP, CH // DP, CH), F32),
            pltpu.VMEM((CH // DP, CH), F32),
            pltpu.VMEM((DP, CH // DP, CH), F32),
            pltpu.VMEM((CH, CH), F32),
            pltpu.VMEM((CH, CH), F32),
            dma((10,)),
            dma((4 * ROW,)),
            dma((4 * ROW,)),
            dma((4 * ROW,)),
            dma((4 * ROW,)),
            dma((4,)),
            dma((4,)),
            dma((8,)),
            dma((8,)),
            dma((DP,)),
            dma((DP,)),
            dma((DP,)),
            dma((DP,)),
        ],
        compiler_params=pltpu.CompilerParams(
            collective_id=0, has_side_effects=True, vmem_limit_bytes=52 * 1024 * 1024
        ),
    )(
        counts.T, keep_count, tile_list, radius[0], sky_image, wave_dual, rank_dual, data_dual[0],
        observed[0], degrid.reshape(SLOTS, VIS, PIX),
    )
    return outs[0], outs[1], outs[2], outs[3][None]


def solution(mesh):
    return jax.shard_map(
        per_device,
        mesh=mesh,
        in_specs=(
            P("dp", "facet", None),
            P("dp", "facet", None),
            P("dp", "facet", None),
            P("facet", "dp", None, None),
            P("facet", "dp", None, None),
            P("facet", "dp", None),
            P("facet", "dp", None, None, None),
            P(None, "dp", None),
            P(None, "dp"),
            P("facet"),
        ),
        out_specs=(
            P("dp", "facet", None),
            P("dp", "facet", None),
            P("dp", "facet", None),
            P("facet", "dp", None, None),
        ),
        check_vma=False,
    )
```

```python
import jax
import jax.numpy as jnp
from jax import lax
from jax.experimental import pallas as pl
from jax.experimental.pallas import tpu as pltpu
from jax.sharding import PartitionSpec as P

MESH = pl.DeviceIdType.MESH
F32 = jnp.float32
BF16 = jnp.bfloat16
HIGH = lax.Precision.HIGHEST

TAPS = (-0.12940952255126037, -0.2241438680420134, 0.8365163037378079, -0.48296291314453416)
FACETS = 16
DP = 8
CAP = 3
SLOTS = 48
TILES = 8
PIX = 128
CH = 256
VIS = 1024
H = 16
W = 64
HALF = 128
ROW = 8
EDGE = 8


def newton_scales(kappa, steps):
    start = 2.0 / (1.0 + kappa)
    rho = (kappa - 1.0) / (kappa + 1.0)
    scales = []
    for _ in range(steps):
        scales.append(2.0 / (2.0 - rho * rho))
        rho = rho * rho / (2.0 - rho * rho)
    return start, scales


START, SCALES = newton_scales(65.0, 8)


def halves(x):
    high = x.astype(BF16)
    return high, (x - high.astype(F32)).astype(BF16)


def dot3(a, b):
    (ah, al), (bh, bl) = halves(a), halves(b)
    return (
        jnp.dot(ah, bl, preferred_element_type=F32)
        + jnp.dot(al, bh, preferred_element_type=F32)
        + jnp.dot(ah, bh, preferred_element_type=F32)
    )


def column_at(i, me):
    x, c = (me // 2) % 4, me % 2
    k = i // 2
    hop = 1 + k + (k * (3 - k) // 2) * (3 - 2 * k)
    return ((x + hop) % 4) * 2 + (c + 1 - i % 2) % 2


def match_table(source, value, target):
    lane = lax.broadcasted_iota(jnp.int32, (FACETS, SLOTS // 2), 1)
    seen = jnp.zeros((FACETS, 1), jnp.int32)
    values = [jnp.zeros((FACETS, 1), jnp.int32)] * CAP
    there = [jnp.zeros((FACETS, 1), jnp.int32)] * CAP
    for b in range(2):
        match = jnp.where(source[b] == target, 1, 0)
        before = jnp.broadcast_to(seen, match.shape)
        for s in range(SLOTS // 2 - 1):
            before = before + jnp.where(lane > s, match[:, s : s + 1], 0)
        seen = seen + jnp.sum(match, axis=1, keepdims=True)
        for j in range(CAP):
            chosen = jnp.where(before == j, match, 0)
            values[j] = values[j] + jnp.sum(chosen * value[b], axis=1, keepdims=True)
            there[j] = there[j] + jnp.sum(chosen, axis=1, keepdims=True)
    return values, there


def kernel(
    counts, keep, tiles_in, radius, sky_h, wave_h, rank_h, dual_h, obs_h, deg_h,
    sky_o, wave_o, rank_o, data_o,
    deg, dual, obs, sky, rank, wpad, epad, half, send1, recv1, ysend, yrecv, send2, recv2, bar, pbar_0, pbar_1,
    tcat, acc, acr, acr2, cols, synth, mixed, pick, tabv, tab, gram, gpart, gsend, gfull, amat, inv,
    lsem, s1, r1, s2, r2, ys, yr, hs, hr, gs, gr, as_, ar,
):
    me = lax.axis_index("facet")
    dp = lax.axis_index("dp")
    pbar = (pbar_0, pbar_1)
    mrow, mcol = me // ROW, me % ROW
    orow = 1 - mrow
    partner = orow * ROW + mcol

    def local(n, src, dst):
        copy = pltpu.make_async_copy(src, dst, lsem.at[n])
        copy.start()
        return copy

    get_dual = local(1, dual_h, dual)
    get_deg = [
        local(2 + n, deg_h.at[pl.ds(n * 12, 12)], deg.at[pl.ds(n * 12, 12)]) for n in range(4)
    ]
    barrier = pltpu.get_barrier_semaphore()

    def greet(axis, to):
        pl.semaphore_signal(barrier, inc=1, device_id={axis: to}, device_id_type=MESH)

    def greet_row(i, carry):
        greet("facet", mrow * ROW + column_at(i, me))
        return carry

    def greet_dp(i, carry):
        greet("dp", (dp + 1 + i) % DP)
        return carry

    down, up = (dp + 1) % DP, (dp + DP - 1) % DP
    right, left = (me + 1) % FACETS, (me + FACETS - 1) % FACETS
    lax.fori_loop(0, ROW - 1, greet_row, 0)
    lax.fori_loop(0, DP - 1, greet_dp, 0)
    greet("facet", partner)
    greet("facet", right)
    greet("facet", left)

    lane24 = lax.broadcasted_iota(jnp.int32, (1, SLOTS // 2), 1)
    rows16 = lax.broadcasted_iota(jnp.int32, (FACETS, 1), 0)
    mine, slot, workers, local_tile = [], [], [], []
    for b in range(2):
        line = tiles_in[pl.ds(me, 1), b, :]
        line = jnp.where(lane24 < counts[b, me], line // TILES, -1)
        mine.append(jnp.broadcast_to(line, (FACETS, SLOTS // 2)))
        slot.append(jnp.broadcast_to(lane24 + b * (SLOTS // 2), (FACETS, SLOTS // 2)))
        eight = tiles_in[pl.ds(pl.multiple_of(mrow * ROW, ROW), ROW), b, :]
        both = jnp.concatenate([eight, eight], axis=0)
        limit = jnp.zeros((FACETS, 1), jnp.int32)
        for n in range(ROW):
            limit = jnp.where(rows16 % ROW == n, counts[b, mrow * ROW + n], limit)
        workers.append(jnp.where(lane24 < limit, both // TILES, -1))
        local_tile.append(both % TILES)
    slots, slots_there = match_table(mine, slot, rows16)
    tiles, tiles_there = match_table(workers, local_tile, jnp.where(rows16 < ROW, partner, me))
    lanes = lax.broadcasted_iota(jnp.int32, (FACETS, 128), 1)
    table = jnp.zeros((FACETS, 128), jnp.int32)
    for n, column in enumerate(slots + slots_there + tiles + tiles_there):
        table = jnp.where(lanes == n, column, table)
    tabv[...] = table
    put_tab = pltpu.make_async_copy(tabv, tab, lsem.at[9])
    put_tab.start()

    wide = ROW * CAP * 16
    row = lax.broadcasted_iota(jnp.int32, (TILES * 16, wide), 0)
    lane = lax.broadcasted_iota(jnp.int32, (TILES * 16, wide), 1)
    lane8 = lax.broadcasted_iota(jnp.int32, (ROW, wide), 1)
    row8 = lax.broadcasted_iota(jnp.int32, (ROW, wide), 0)
    for kind in range(2):
        named = jnp.zeros((1, wide), jnp.int32)
        for j in range(CAP):
            code = jnp.where(tiles_there[j] > 0, tiles[j] + 1, 0)[kind * ROW : (kind + 1) * ROW]
            here = (lane8 // 48 == row8) & ((lane8 % 48) // 16 == j)
            named = named + jnp.sum(jnp.where(here, code, 0), axis=0, keepdims=True)
        hit = (named - 1 == row // 16) & (row % 16 == lane % 16)
        pick[kind] = jnp.where(hit, 1.0, 0.0).astype(BF16)

    @pl.when(dp == 0)
    def _():
        wpad[0:2] = jnp.zeros((2, W, CH), F32)
        epad[0:1] = jnp.zeros((1, W, CH), F32)

    @pl.when(dp == DP - 1)
    def _():
        wpad[18:19] = jnp.zeros((1, W, CH), F32)
        epad[17:19] = jnp.zeros((2, W, CH), F32)

    @pl.when(me == 0)
    def _():
        cols[4:6] = jnp.zeros((2, H, CH), F32)
        cols[10:11] = jnp.zeros((1, H, CH), F32)

    @pl.when(me == FACETS - 1)
    def _():
        cols[6:7] = jnp.zeros((1, H, CH), F32)
        cols[12:14] = jnp.zeros((2, H, CH), F32)

    pl.semaphore_wait(barrier, ROW - 1 + DP - 1 + 3)

    def hop(n, src, dst, axis, to):
        return pltpu.make_async_remote_copy(
            src_ref=src, dst_ref=dst, send_sem=hs.at[n], recv_sem=hr.at[n],
            device_id={axis: to}, device_id_type=MESH,
        )

    hops = (
        (hop(0, wpad.at[pl.ds(16, 2)], wpad.at[pl.ds(0, 2)], "dp", down), dp < DP - 1, dp > 0),
        (hop(1, wpad.at[pl.ds(2, 1)], wpad.at[pl.ds(18, 1)], "dp", up), dp > 0, dp < DP - 1),
        (hop(2, cols.at[pl.ds(0, 2)], cols.at[pl.ds(4, 2)], "facet", right), me < FACETS - 1, me > 0),
        (hop(3, cols.at[pl.ds(2, 1)], cols.at[pl.ds(6, 1)], "facet", left), me > 0, me < FACETS - 1),
        (hop(4, epad.at[pl.ds(16, 1)], epad.at[pl.ds(0, 1)], "dp", down), dp < DP - 1, dp > 0),
        (hop(5, epad.at[pl.ds(1, 2)], epad.at[pl.ds(17, 2)], "dp", up), dp > 0, dp < DP - 1),
        (hop(6, cols.at[pl.ds(7, 1)], cols.at[pl.ds(10, 1)], "facet", right), me < FACETS - 1, me > 0),
        (hop(7, cols.at[pl.ds(8, 2)], cols.at[pl.ds(12, 2)], "facet", left), me > 0, me < FACETS - 1),
    )

    def hop_start(n):
        copy, sends, _ = hops[n]

        @pl.when(sends)
        def _():
            copy.start()

    def hop_arrive(n):
        copy, _, receives = hops[n]

        @pl.when(receives)
        def _():
            copy.wait_recv()

    def hop_left(n):
        copy, sends, _ = hops[n]

        @pl.when(sends)
        def _():
            copy.wait_send()

    get_dual.wait()
    half[...] = dual[...].astype(BF16)
    put_tab.wait()
    for copy in get_deg:
        copy.wait()
    get_wave = local(0, wave_h, wpad.at[pl.ds(2, H)])
    get_sky = local(6, sky_h, sky)
    get_rank = local(7, rank_h, rank)
    get_obs = local(8, obs_h, obs)

    def row_copy(sends, src, dst, to, sent, came):
        return pltpu.make_async_remote_copy(
            src_ref=src, dst_ref=dst, send_sem=sends[0].at[sent], recv_sem=sends[1].at[came],
            device_id={"facet": mrow * ROW + to}, device_id_type=MESH,
        )

    def target_row(kind):
        return mrow if kind == 1 else orow

    def out_1(g, kind, to):
        return row_copy(
            (s1, r1), send1.at[g, pl.ds((target_row(kind) * ROW + to) * CAP, CAP)],
            recv1.at[g, pl.ds((kind * ROW + mcol) * CAP, CAP)], to,
            (g * 2 + kind) * ROW + to, (g * 2 + kind) * ROW + mcol,
        )

    def in_1(g, kind, source):
        region = recv1.at[g, pl.ds((kind * ROW + source) * CAP, CAP)]
        n = (g * 2 + kind) * ROW + source
        return row_copy((s1, r1), region, region, source, n, n)

    def out_2(g, kind, to):
        return row_copy(
            (s2, r2), send2.at[g, pl.ds((kind * ROW + to) * CAP, CAP)],
            recv2.at[g, pl.ds((target_row(kind) * ROW + mcol) * CAP, CAP)], to,
            (g * 2 + kind) * ROW + to, (g * 2 + kind) * ROW + mcol,
        )

    def in_2(g, kind, source):
        region = recv2.at[g, pl.ds((target_row(kind) * ROW + source) * CAP, CAP)]
        n = (g * 2 + kind) * ROW + source
        return row_copy((s2, r2), region, region, source, n, n)

    def across(g, n, src, dst):
        return pltpu.make_async_remote_copy(
            src_ref=src.at[g], dst_ref=dst, send_sem=ys.at[n * 2 + g], recv_sem=yr.at[n * 2 + g],
            device_id={"facet": partner}, device_id_type=MESH,
        )

    def each(fn):
        def step(i, carry):
            fn(column_at(i, me))
            return carry

        lax.fori_loop(0, ROW - 1, step, 0)

    for kind in range(2):
        def adjoint(i, carry, kind=kind):
            to = column_at(i, me)
            facet = target_row(kind) * ROW + to
            for j in range(CAP):
                at = tab[facet, j]
                part = lax.dot_general(
                    deg[at], half[jnp.where(at < SLOTS // 2, 0, 1)],
                    (((0,), (0,)), ((), ())), preferred_element_type=F32,
                )
                part = (part * tab[facet, CAP + j].astype(F32)).astype(BF16)
                send1[0, facet * CAP + j] = part[:, :HALF]
                send1[1, facet * CAP + j] = part[:, HALF:]

            @pl.when(i < ROW - 1)
            def _():
                out_1(0, kind, to).start()

            return carry

        lax.fori_loop(0, ROW, adjoint, 0)
    for g in range(2):
        for kind in range(2):
            recv1[g, pl.ds((kind * ROW + mcol) * CAP, CAP)] = send1[
                g, pl.ds((target_row(kind) * ROW + mcol) * CAP, CAP)
            ]

    get_wave.wait()
    hop_start(0)
    hop_start(1)

    hop_arrive(0)
    hop_arrive(1)

    def synth_rows(i, carry):
        total = TAPS[0] * wpad[i + 3]
        for a in range(1, 4):
            total = total + TAPS[a] * wpad[i + 3 - a]
        acr[i, EDGE : EDGE + W] = total
        return carry

    lax.fori_loop(0, H, synth_rows, 0)
    for q in range(2):
        cols[q] = acr[:, EDGE + W - 2 + q, :]
    cols[2] = acr[:, EDGE, :]
    hop_start(2)
    hop_start(3)
    get_sky.wait()
    get_rank.wait()
    hop_arrive(2)
    hop_arrive(3)
    for q in range(2):
        acr[:, EDGE - 2 + q, :] = cols[4 + q]
    acr[:, EDGE + W, :] = cols[6]

    def synth_cols(i, carry):
        total = TAPS[0] * acr[i, EDGE + 1 : EDGE + 1 + W]
        for a in range(1, 4):
            total = total + TAPS[a] * acr[i, EDGE + 1 - a : EDGE + 1 - a + W]
        synth[i] = total
        return carry

    lax.fori_loop(0, H, synth_cols, 0)

    def follow(kind, to):
        out_1(0, kind, to).wait_send()
        out_1(1, kind, to).start()

    for kind in range(2):
        each(lambda to, kind=kind: follow(kind, to))

    entries = ROW * CAP

    def relay(g):
        each(lambda source: in_1(g, 0, source).wait_recv())

        def step(i, carry):
            at = pl.ds(pl.multiple_of(i * 16, 16), 16)
            part = recv1[g, 0:entries, at, :].reshape(entries * 16, HALF)
            total = jnp.dot(pick[0], part, preferred_element_type=F32)
            ysend[g, :, at, :] = total.astype(BF16).reshape(TILES, 16, HALF)
            return carry

        lax.fori_loop(0, 8, step, 0)
        across(g, 0, ysend, yrecv.at[g]).start()

    def update(g):
        each(lambda source: in_1(g, 1, source).wait_recv())
        across(g, 0, ysend, yrecv.at[g]).wait_recv()
        ch = slice(g * HALF, (g + 1) * HALF)

        def step(i, carry):
            at = pl.ds(pl.multiple_of(i * 16, 16), 16)
            part = recv1[g, entries : 2 * entries, at, :].reshape(entries * 16, HALF)
            back = jnp.dot(pick[1], part, preferred_element_type=F32)
            back = back + yrecv[g, :, at, :].reshape(TILES * 16, HALF).astype(F32)
            for r in range(2):
                y = r * 8 + i
                held = sky[y, :, ch]
                gradient = back[r * W : (r + 1) * W] + synth[y, :, ch] + rank[y, :, ch]
                after = jnp.maximum(held - 0.5 * gradient, 0.0)
                extrap = 2.0 * after - held
                sky_o[y, :, ch] = after
                epad[y + 1, :, ch] = extrap
                mixed[pl.ds(pl.multiple_of(y * W, W), W), ch] = rank[y, :, ch] + 0.5 * extrap
                bar[g, r * 4 : r * 4 + 4, at, :] = extrap.astype(BF16).reshape(4, 16, HALF)
            return carry

        lax.fori_loop(0, 8, step, 0)
        across(g, 1, bar, pbar[g]).start()

    def deal(g, kind):
        held = bar.at[g] if kind == 1 else pbar[g]
        if kind == 0:
            across(g, 1, bar, pbar[g]).wait_recv()

        def step(i, carry):
            to = column_at(i, me)
            for j in range(CAP):
                tile = held[tab[kind * ROW + to, 2 * CAP + j]]
                send2[g, (kind * ROW + to) * CAP + j] = tile

            @pl.when(i < ROW - 1)
            def _():
                out_2(g, kind, to).start()

            return carry

        lax.fori_loop(0, ROW, step, 0)
        recv2[g, pl.ds((target_row(kind) * ROW + mcol) * CAP, CAP)] = send2[
            g, pl.ds((kind * ROW + mcol) * CAP, CAP)
        ]

    def forward(g, kind):
        each(lambda source: in_2(g, kind, source).wait_recv())
        first = target_row(kind) * ROW

        def spread(i, carry):
            for j in range(CAP):
                at = tab[first + i, j]
                live = tab[first + i, CAP + j]
                tile = recv2[g, (first + i) * CAP + j].astype(F32)
                for b in range(2):
                    mask = live * (jnp.where(at < SLOTS // 2, 1 - b, b))
                    tcat[i * CAP + j, :, b * HALF : (b + 1) * HALF] = (
                        tile * mask.astype(F32)
                    ).astype(BF16)
            return carry

        lax.fori_loop(0, ROW, spread, 0)

        def multiply(i, carry):
            at = pl.ds(pl.multiple_of(i * 512, 512), 512)
            weights = jnp.concatenate(
                [deg[tab[first + n // CAP, n % CAP], at, :] for n in range(entries)], axis=1
            )
            product = jnp.dot(
                weights, tcat[...].reshape(entries * PIX, CH), preferred_element_type=F32
            )
            if kind == 1:
                acc[g, at, :] = product
                return carry
            product = acc[g, at, :] + product
            ch = slice(g * HALF, (g + 1) * HALF)
            squares = []
            for b in range(2):
                miss = (
                    dual[b, at, ch]
                    + product[:, b * HALF : (b + 1) * HALF]
                    - obs[b, at, ch].astype(F32)
                )
                data_o[b, at, ch] = miss
                squares.append(carry[b] + jnp.sum(miss * miss, axis=0, keepdims=True))
            return tuple(squares)

        if kind == 1:
            lax.fori_loop(0, 2, multiply, 0)
            return
        zero = jnp.zeros((1, HALF), F32)
        totals = lax.fori_loop(0, 2, multiply, (zero, zero))
        ch = slice(g * HALF, (g + 1) * HALF)
        for b in range(2):
            size = jnp.sqrt(totals[b] + 1e-06)
            shrink = jnp.maximum(0.0, 1.0 - radius[pl.ds(b, 1), ch] / size)

            def scale_rows(i, carry, b=b, shrink=shrink):
                at = pl.ds(pl.multiple_of(i * 128, 128), 128)
                data_o[b, at, ch] = data_o[b, at, ch] * shrink
                return carry

            lax.fori_loop(0, 8, scale_rows, 0)

    get_obs.wait()
    relay(0)
    update(0)
    deal(0, 1)
    relay(1)
    deal(0, 0)
    update(1)
    deal(1, 1)
    hop_start(4)
    hop_start(5)

    rows_d = CH // DP
    high, low = halves(mixed[...])
    first = lax.dot_general(high, high, (((0,), (0,)), ((), ())), preferred_element_type=F32)
    second = lax.dot_general(high, low, (((0,), (0,)), ((), ())), preferred_element_type=F32)
    gram[...] = (first + (second + second.T)).reshape(DP, rows_d, CH)

    def gram_out(to):
        return pltpu.make_async_remote_copy(
            src_ref=gram.at[to], dst_ref=gpart.at[dp], send_sem=gs.at[to], recv_sem=gr.at[dp],
            device_id={"dp": to}, device_id_type=MESH,
        )

    def gram_in(source):
        return pltpu.make_async_remote_copy(
            src_ref=gram.at[source], dst_ref=gpart.at[source], send_sem=gs.at[source],
            recv_sem=gr.at[source], device_id={"dp": source}, device_id_type=MESH,
        )

    def all_out(to):
        return pltpu.make_async_remote_copy(
            src_ref=gsend, dst_ref=gfull.at[dp], send_sem=as_.at[to], recv_sem=ar.at[dp],
            device_id={"dp": to}, device_id_type=MESH,
        )

    def all_in(source):
        return pltpu.make_async_remote_copy(
            src_ref=gsend, dst_ref=gfull.at[source], send_sem=as_.at[source],
            recv_sem=ar.at[source], device_id={"dp": source}, device_id_type=MESH,
        )

    def others(fn):
        def step(i, carry):
            fn((dp + 1 + i) % DP)
            return carry

        lax.fori_loop(0, DP - 1, step, 0)

    others(lambda d: gram_out(d).start())
    gpart[dp] = gram[dp]

    forward(0, 1)
    deal(1, 0)

    hop_arrive(4)
    hop_arrive(5)

    def analysis_rows(i, carry):
        total = TAPS[0] * epad[i]
        for a in range(1, 4):
            total = total + TAPS[a] * epad[i + a]
        acr2[i, EDGE : EDGE + W] = total
        return carry

    lax.fori_loop(0, H, analysis_rows, 0)
    cols[7] = acr2[:, EDGE + W - 1, :]
    for q in range(2):
        cols[8 + q] = acr2[:, EDGE + q, :]
    hop_start(6)
    hop_start(7)

    others(lambda d: gram_in(d).wait_recv())
    total = gpart[0]
    for d in range(1, DP):
        total = total + gpart[d]
    gsend[...] = total
    others(lambda d: all_out(d).start())
    gfull[dp] = total

    forward(0, 0)
    hop_arrive(6)
    hop_arrive(7)
    acr2[:, EDGE - 1, :] = cols[10]
    for q in range(2):
        acr2[:, EDGE + W + q, :] = cols[12 + q]

    def analysis_cols(i, carry):
        total = TAPS[0] * acr2[i, EDGE - 1 : EDGE - 1 + W]
        for a in range(1, 4):
            total = total + TAPS[a] * acr2[i, EDGE - 1 + a : EDGE - 1 + a + W]
        wave_o[i] = jnp.clip(wpad[i + 2] + 0.5 * total, -1.0, 1.0)
        return carry

    lax.fori_loop(0, H, analysis_cols, 0)

    forward(1, 1)
    others(lambda d: all_in(d).wait_recv())
    full = gfull[...].reshape(CH, CH)
    diag = lax.broadcasted_iota(jnp.int32, (CH, CH), 0) == lax.broadcasted_iota(jnp.int32, (CH, CH), 1)
    eye = jnp.where(diag, 1.0, 0.0)
    trace = jnp.sum(jnp.sum(full * eye, axis=1, keepdims=True), axis=0, keepdims=True)
    level = (trace + 1e-06) / keep[0].astype(F32)
    matrix = eye + full / level
    amat[...] = matrix
    inv[...] = (SCALES[0] * START) * (2.0 * eye - START * matrix)
    coarse = matrix.astype(BF16)
    x = inv[...]
    for scale in SCALES[1:4]:
        residual = 2.0 * eye - jnp.dot(coarse, x.astype(BF16), preferred_element_type=F32)
        x = scale * jnp.dot(x.astype(BF16), residual.astype(BF16), preferred_element_type=F32)
    fine = (matrix - coarse.astype(F32)).astype(BF16)
    x = x.astype(BF16)
    residual = eye - (
        jnp.dot(coarse, x, preferred_element_type=F32) + jnp.dot(fine, x, preferred_element_type=F32)
    )
    inv[...] = x.astype(F32) + jnp.dot(x, residual.astype(BF16), preferred_element_type=F32)
    x = inv[...]
    inv[...] = x + dot3(x, eye - dot3(amat[...], x))
    x = inv[...]
    residual = eye - dot3(amat[...], x)
    inv[...] = x + jnp.dot(x.astype(BF16), residual.astype(BF16), preferred_element_type=F32)

    def apply_rank(i, carry):
        at = pl.ds(pl.multiple_of(i * 256, 256), 256)
        out = dot3(mixed[at], inv[...])
        rank_o[pl.ds(i * 4, 4)] = out.reshape(4, W, CH)
        return carry

    lax.fori_loop(0, 4, apply_rank, 0)

    forward(1, 0)

    for g in range(2):
        for kind in range(2):
            if g == 1:
                each(lambda to, kind=kind: out_1(1, kind, to).wait_send())
            each(lambda to, g=g, kind=kind: out_2(g, kind, to).wait_send())
        across(g, 0, ysend, yrecv.at[g]).wait_send()
        across(g, 1, bar, pbar[g]).wait_send()
    others(lambda d: gram_out(d).wait_send())
    others(lambda d: all_out(d).wait_send())
    for n in range(8):
        hop_left(n)


def per_device(
    sky_image, wave_dual, rank_dual, data_dual, observed, radius, degrid, tile_list, counts, keep_count
):
    hbm = pl.BlockSpec(memory_space=pl.ANY)
    vmem = pl.BlockSpec(memory_space=pltpu.VMEM)
    smem = pl.BlockSpec(memory_space=pltpu.SMEM)
    dma = pltpu.SemaphoreType.DMA
    outs = pl.pallas_call(
        kernel,
        out_shape=(
            pltpu.VMEM((H, W, CH), F32), pltpu.VMEM((H, W, CH), F32), pltpu.VMEM((H, W, CH), F32),
            pltpu.VMEM((2, VIS, CH), F32),
        ),
        in_specs=[smem, smem, vmem, vmem] + [hbm] * 6,
        out_specs=[vmem] * 4,
        scratch_shapes=[
            pltpu.VMEM((SLOTS, VIS, PIX), BF16),
            pltpu.VMEM((2, VIS, CH), F32),
            pltpu.VMEM((2, VIS, CH), BF16),
            pltpu.VMEM((H, W, CH), F32),
            pltpu.VMEM((H, W, CH), F32),
            pltpu.VMEM((H + 3, W, CH), F32),
            pltpu.VMEM((H + 3, W, CH), F32),
            pltpu.VMEM((2, VIS, CH), BF16),
            pltpu.VMEM((2, SLOTS, PIX, HALF), BF16),
            pltpu.VMEM((2, SLOTS, PIX, HALF), BF16),
            pltpu.VMEM((2, TILES, PIX, HALF), BF16),
            pltpu.VMEM((2, TILES, PIX, HALF), BF16),
            pltpu.VMEM((2, SLOTS, PIX, HALF), BF16),
            pltpu.VMEM((2, SLOTS, PIX, HALF), BF16),
            pltpu.VMEM((2, TILES, PIX, HALF), BF16),
            pltpu.VMEM((TILES, PIX, HALF), BF16),
            pltpu.VMEM((TILES, PIX, HALF), BF16),
            pltpu.VMEM((ROW * CAP, PIX, CH), BF16),
            pltpu.VMEM((2, VIS, CH), F32),
            pltpu.VMEM((H, W + 2 * EDGE, CH), F32),
            pltpu.VMEM((H, W + 2 * EDGE, CH), F32),
            pltpu.VMEM((14, H, CH), F32),
            pltpu.VMEM((H, W, CH), F32),
            pltpu.VMEM((H * W, CH), F32),
            pltpu.VMEM((2, TILES * 16, ROW * CAP * 16), BF16),
            pltpu.VMEM((FACETS, 128), jnp.int32),
            pltpu.SMEM((FACETS, 128), jnp.int32),
            pltpu.VMEM((DP, CH // DP, CH), F32),
            pltpu.VMEM((DP, CH // DP, CH), F32),
            pltpu.VMEM((CH // DP, CH), F32),
            pltpu.VMEM((DP, CH // DP, CH), F32),
            pltpu.VMEM((CH, CH), F32),
            pltpu.VMEM((CH, CH), F32),
            dma((10,)),
            dma((4 * ROW,)),
            dma((4 * ROW,)),
            dma((4 * ROW,)),
            dma((4 * ROW,)),
            dma((4,)),
            dma((4,)),
            dma((8,)),
            dma((8,)),
            dma((DP,)),
            dma((DP,)),
            dma((DP,)),
            dma((DP,)),
        ],
        compiler_params=pltpu.CompilerParams(
            collective_id=0, has_side_effects=True, vmem_limit_bytes=52 * 1024 * 1024
        ),
    )(
        counts.T, keep_count, tile_list, radius[0], sky_image, wave_dual, rank_dual, data_dual[0],
        observed[0], degrid.reshape(SLOTS, VIS, PIX),
    )
    return outs[0], outs[1], outs[2], outs[3][None]


def solution(mesh):
    return jax.shard_map(
        per_device,
        mesh=mesh,
        in_specs=(
            P("dp", "facet", None),
            P("dp", "facet", None),
            P("dp", "facet", None),
            P("facet", "dp", None, None),
            P("facet", "dp", None, None),
            P("facet", "dp", None),
            P("facet", "dp", None, None, None),
            P(None, "dp", None),
            P(None, "dp"),
            P("facet"),
        ),
        out_specs=(
            P("dp", "facet", None),
            P("dp", "facet", None),
            P("dp", "facet", None),
            P("facet", "dp", None, None),
        ),
        check_vma=False,
    )
```
